128 devices in a mesh: expert: 32 (over z, y, core), tensor: 4 (over x).
Axes of the slice: x: 4, y: 4, z: 4, core: 2. Of those that a mesh axis runs over, the one named last changes fastest.
Arguments:
- activations: bfloat16 [4096, 7168], P('expert', 'tensor'), may hold values from -6 to 6
- cotangent: bfloat16 [4096, 7168], P('expert', 'tensor'), may hold values from -6 to 6
- expert_ids: int32 [4096, 8], P('expert'), may hold values from 0 to 31, all different within a row; in each aligned block of 128 rows (0 to 127, 128 to 255, ...) at most 40 rows name the same one
- combine: float32 [4096, 8], P('expert'), may hold values from 0.1 to 0.6
- log_ratio: float32 [4096], P('expert'), may hold values from -3 to 3
- valid_mask: int32 [4096], P('expert'), may hold values from 0 to 1, as said below
- segment_ids: int32 [4096], P('expert'), may hold values from 0 to 63, as said below
- w_gate: bfloat16 [32, 7168, 1024], P('expert', 'tensor'), may hold values from -0.0625 to 0.0625
- w_up: bfloat16 [32, 7168, 1024], P('expert', 'tensor'), may hold values from -0.0625 to 0.0625
- w_down: bfloat16 [32, 1024, 7168], P('expert', None, 'tensor'), may hold values from -0.1875 to 0.1875
Outputs:
- input_grad: bfloat16 [4096, 7168], P('expert', 'tensor')
- down_grad: bfloat16 [32, 1024, 7168], P('expert', None, 'tensor')
The draws below stay inside these ranges and needn't reach their ends.
Inputs may be any that keep to these rules, and one draw needn't show every extreme that they name: `expert_ids`: among the 128 tokens of one index of expert, each expert is named at most 40 times. `valid_mask`: 0 at the last of the 128 tokens of every index of expert. `segment_ids`: never falling; no sequence begins at the first token of an index of expert other than index 0; each sequence has 1 to 254 tokens.
All inputs are finite; a program needn't handle non-finite values.
Results may differ from the reference program's by a relative error of at most 0.0064.
Values may be sent and summed in bfloat16 or wider, within the bound.
A program may use at most 128 MiB of HBM per device.

```python
import math
import jax
import jax.numpy as jnp
import numpy as np
from jax import lax

D = 7168
FFW = 1024
TOPK = 8
TOK_DEV = 128
EXPERTS = 32
CAP = 40
TOKENS = 4096


def draw_valid_mask(key, part):
    key = jax.random.fold_in(key, 7)
    ticket = jax.random.randint(key, (TOKENS,), 0, 2 * TOKENS)
    places = jnp.arange(TOKENS, dtype=jnp.int32)
    chosen = (ticket < TOKENS // 2 + places).astype(jnp.int32)
    return chosen * (places % TOK_DEV != TOK_DEV - 1).astype(jnp.int32)


def draw_segment_ids(key, part):
    key = jax.random.fold_in(key, 11)
    first_key, second_key = jax.random.split(key)
    groups = TOKENS // TOK_DEV
    first = jax.random.randint(first_key, (groups,), 0, TOK_DEV - 2)
    second = jax.random.randint(second_key, (groups,), 0, TOK_DEV - 2)
    lower_cut = 1 + jnp.minimum(first, second)
    upper_cut = 2 + jnp.maximum(first, second)
    local = jnp.arange(TOK_DEV, dtype=jnp.int32)[None, :]
    passed = (local >= lower_cut[:, None]).astype(jnp.int32) + (local >= upper_cut[:, None]).astype(jnp.int32)
    labels = 2 * jnp.arange(groups, dtype=jnp.int32)[:, None] + passed - 1
    return jnp.maximum(labels, 0).reshape(-1).astype(jnp.int32)


def block_levels(own_key, dims, cuts, smallest, top_value):
    loudness, own = 1.0, jax.random.fold_in(own_key, 6)
    for dim, shards_of in cuts:
        draws = jnp.exp(jax.random.uniform(jax.random.fold_in(own, dim), (shards_of,), jnp.float32, smallest / len(cuts), top_value / len(cuts)))
        loudness = loudness * jnp.repeat(draws, dims[dim] // shards_of).reshape([-1 if axis == dim else 1 for axis in range(len(dims))])
    return loudness


def deal_out(own_key, own, number, rows, count, top, reach, skew):
    ranking = jax.random.permutation(own_key, count)
    crowded, usual = shares(count, rows * top, reach, skew, True), shares(count, rows * top, reach, skew, False)
    places = jnp.arange(count)

    def named(sizes, rotation):
        used = int((sizes > 0).sum())
        fixed = max(1, used // 4)
        shifted = fixed + (places - fixed + rotation * (used - fixed)) % max(1, count - fixed)
        return jnp.zeros((count,), jnp.int32).at[ranking[jnp.where(places < fixed, places, shifted)]].set(jnp.asarray(sizes, jnp.int32))

    sizes = jnp.where(number % 4 == 0, named(crowded, number // 4), named(usual, number - number // 4 - 1))
    mixed = jax.random.permutation(jax.random.fold_in(own, 3), count)
    giver, receiver = mixed[0:count // 2 * 2:2], mixed[1:count // 2 * 2:2]
    room = jnp.minimum(sizes[giver] - 1, reach - sizes[receiver]) // 2
    room = jnp.where((giver == ranking[0]) | (receiver == ranking[0]) | (sizes[receiver] == 0), 0, jnp.maximum(room, 0))
    shifted = jax.random.randint(jax.random.fold_in(own, 4), (count // 2,), 0, 1 << 20) % (room + 1)
    sizes = sizes.at[giver].add(-shifted).at[receiver].add(shifted)
    items = jnp.searchsorted(jnp.cumsum(sizes), jnp.arange(rows * top), side="right").astype(jnp.int32)
    grid = items.reshape(top, rows).T
    grid = grid[jax.random.permutation(jax.random.fold_in(own, 1), rows)]
    rotation = jax.random.randint(jax.random.fold_in(own, 2), (rows, 1), 0, top)
    return jnp.take_along_axis(grid, (jnp.arange(top)[None, :] + rotation) % top, axis=1)


def shares(number_of, total, limit, lean, full):
    weights = [(1 << 20) // math.isqrt(grade ** lean) + 1 for grade in range(1, number_of + 1)]
    largest = limit if full else min(limit, max(-(-total // number_of), total * weights[0] // sum(weights)))
    least = 1 if total - largest >= number_of - 1 else 0
    counts, surplus = [largest] + [least] * (number_of - 1), total - largest - least * (number_of - 1)
    while surplus > 0:
        candidates = [i for i in range(1, number_of) if counts[i] < largest] or [i for i in range(1, number_of) if counts[i] < limit]
        whole, budget = sum([weights[i] for i in candidates]), surplus
        for i in candidates:
            more = min(limit - counts[i], max(1, budget * weights[i] // whole), surplus)
            counts[i] = counts[i] + more
            surplus = surplus - more
    return np.array(counts)


def normal_values(rng, shape, deviation, bound, cuts=(), kind=jnp.bfloat16):
    loudness = block_levels(rng, shape, cuts, -0.22, 0.18) if cuts else 1.0
    result = jax.random.normal(rng, shape, jnp.float32) * deviation * loudness
    return jnp.minimum(jnp.maximum(result, -bound), bound).astype(kind)


def setup_inputs(seed: int = 0) -> dict:
    keys = jax.random.split(jax.random.key(seed), 11)
    activations = normal_values(keys[0], (TOKENS, D), 1.0, 6.0, ((0, 32), (1, 4)))
    cotangent = normal_values(keys[1], (TOKENS, D), 1.0, 6.0, ((0, 32), (1, 4)))
    expert_ids_keys = jax.random.split(jax.random.fold_in(keys[2], 1), TOKENS // TOK_DEV)
    expert_ids_turns = jax.random.permutation(jax.random.fold_in(keys[2], 3), TOKENS // TOK_DEV)
    expert_ids = jax.vmap(lambda own, number: deal_out(jax.random.fold_in(keys[2], 2), own, number, TOK_DEV, EXPERTS, TOPK, CAP, 2))(expert_ids_keys, expert_ids_turns).reshape((TOKENS, TOPK))
    combine = jnp.clip(0.1 + 0.5 * jax.random.uniform(keys[3], (TOKENS, TOPK), jnp.float32) ** block_levels(keys[3], (TOKENS, TOPK), ((0, 32),), -0.2, 0.2), 0.1, 0.6)
    log_ratio = normal_values(keys[4], (TOKENS,), 0.5, 3.0, ((0, 32),), jnp.float32)
    valid_mask = draw_valid_mask(jax.random.fold_in(keys[10], 71), 0)
    segment_ids = draw_segment_ids(jax.random.fold_in(keys[10], 71), 0)
    w_gate = normal_values(keys[7], (EXPERTS, D, FFW), D ** -0.5, 0.0625, ((0, 32), (1, 4)))
    w_up = normal_values(keys[8], (EXPERTS, D, FFW), D ** -0.5, 0.0625, ((0, 32), (1, 4)))
    w_down = normal_values(keys[9], (EXPERTS, FFW, D), FFW ** -0.5, 0.1875, ((0, 32), (2, 4)))
    return {"activations": activations, "cotangent": cotangent, "expert_ids": expert_ids, "combine": combine, "log_ratio": log_ratio, "valid_mask": valid_mask, "segment_ids": segment_ids, "w_gate": w_gate, "w_up": w_up, "w_down": w_down}


def pointwise(gate_pre, up_pre, down_pre, scale_rows):
    sigmoid_val = jax.nn.sigmoid(gate_pre)
    activated = gate_pre * sigmoid_val
    slope = sigmoid_val * (1.0 + gate_pre * (1.0 - sigmoid_val))
    scaled_dh = down_pre * scale_rows
    hidden_scaled = (activated * up_pre * scale_rows).astype(jnp.bfloat16)
    grad_gate = (scaled_dh * up_pre * slope).astype(jnp.bfloat16)
    grad_up = (scaled_dh * activated).astype(jnp.bfloat16)
    return hidden_scaled, grad_gate, grad_up


def reference(activations, cotangent, expert_ids, combine, log_ratio, valid_mask, segment_ids, w_gate, w_up, w_down):
    following = jnp.concatenate([segment_ids[1:], jnp.full((1,), -1, jnp.int32)])
    live_mask = jnp.maximum(valid_mask, (following != segment_ids).astype(jnp.int32))
    live_total = jnp.sum(live_mask.astype(jnp.float32))
    factor = TOKENS / live_total
    weight = jnp.minimum(jnp.exp(log_ratio), 2.0) * live_mask.astype(jnp.float32)
    slot_scale = lax.optimization_barrier((combine * weight[:, None]).astype(jnp.bfloat16))
    row_limit = EXPERTS * CAP

    def one_expert(running, inputs):
        expert, gate_mat, up_mat, down_mat = inputs
        chosen = expert_ids == expert
        token_mask = jnp.any(chosen, axis=1)
        token_scale = jnp.sum(jnp.where(chosen, slot_scale.astype(jnp.float32), 0.0), axis=1)
        picked = jnp.nonzero(token_mask, size=row_limit, fill_value=0)[0].astype(jnp.int32)
        in_use = jnp.arange(row_limit, dtype=jnp.int32) < jnp.sum(token_mask.astype(jnp.int32))
        rows_scale = jnp.where(in_use, token_scale[picked], 0.0)[:, None]
        rows_act = activations[picked]
        rows_cot = cotangent[picked]
        gate_pre = jnp.dot(rows_act, gate_mat, preferred_element_type=jnp.float32)
        up_pre = jnp.dot(rows_act, up_mat, preferred_element_type=jnp.float32)
        down_pre = jnp.dot(rows_cot, down_mat.T, preferred_element_type=jnp.float32)
        hidden_scaled, grad_gate, grad_up = pointwise(gate_pre, up_pre, down_pre, rows_scale)
        slot_grad = jnp.dot(grad_gate, gate_mat.T, preferred_element_type=jnp.float32)
        slot_grad = slot_grad + jnp.dot(grad_up, up_mat.T, preferred_element_type=jnp.float32)
        slot_grad = lax.optimization_barrier(slot_grad.astype(jnp.bfloat16))
        running = running.at[picked].add(jnp.where(in_use[:, None], slot_grad.astype(jnp.float32), 0.0))
        down_sum = jnp.dot(hidden_scaled.T, rows_cot, preferred_element_type=jnp.float32)
        return running, (down_sum * factor).astype(jnp.bfloat16)

    start_grad = jnp.zeros((TOKENS, D), jnp.float32)
    experts_list = jnp.arange(EXPERTS, dtype=jnp.int32)
    running, down_grad = lax.scan(one_expert, start_grad, (experts_list, w_gate, w_up, w_down))
    input_grad = (running * factor).astype(jnp.bfloat16)
    return input_grad, down_grad
```

```python
import functools

import jax
import jax.numpy as jnp
from jax import lax
from jax.experimental import pallas as pl
from jax.experimental.pallas import tpu as pltpu
from jax.sharding import PartitionSpec as P

BF = jnp.bfloat16
F32 = jnp.float32
MESH = pl.DeviceIdType.MESH

SIDE = 4
CHIPS = SIDE * SIDE
CAP = 40
TOK = 128
ROWS = 2 * CAP
TOP = 8
GROUP = 2
CHUNKS = CHIPS // GROUP
R = GROUP * ROWS
HID = 128
BLOCK = 2 * TOK + 16

ORDER = [
    (0, 0), (3, 0), (1, 0), (0, 3), (0, 1), (3, 3), (1, 1), (3, 1),
    (1, 3), (2, 0), (0, 2), (3, 2), (2, 3), (1, 2), (2, 1), (2, 2),
]
EVENTS = [
    [(3, 0), (0, 3), (1, 0), (0, 1)],
    [],
    [(3, 3), (2, 0)],
    [(1, 3), (3, 1), (1, 1)],
    [(0, 2)],
    [(2, 3), (2, 1), (3, 2)],
    [(1, 2)],
    [(2, 2)],
]
HALVES = (pl.ds(0, TOK), pl.ds(TOK, BLOCK - TOK))


def dot(a, b, ca, cb):
    return lax.dot_general(a, b, (((ca,), (cb,)), ((), ())), preferred_element_type=F32)


def kernel(
    blk, w_gate, w_up, w_down,
    in_grad, down_grad, gbuf,
    wgu, wd, stage, rowact, rowcot, scl, part, own, r1, r2, ag, hs, rets, retr, dense, sibr, sall,
    dgt, igt, cnt,
    wsem, stsem, gsend, grecv, bsend, brecv, r1s, r1r, r2s, r2r, a1s, a1r, a2s, a2r, rts, rtr,
    css, csr, osem,
):
    e = lax.axis_index("expert")
    x = lax.axis_index("tensor")
    c = lax.rem(e, 2)
    chip = lax.div(e, 2)
    z = lax.div(chip, SIDE)
    y = lax.rem(chip, SIDE)
    width = blk.shape[1]
    right = lax.rem(x + 1, SIDE)
    left = lax.rem(x + SIDE - 1, SIDE)

    def chip_at(dz, dy):
        return lax.rem(z + dz, SIDE) * SIDE + lax.rem(y + dy, SIDE)

    def peer(dz, dy):
        return (chip_at(dz, dy) * 2 + c, x)

    sibling = (chip * 2 + 1 - c, x)

    def zy(da, db):
        return da * (1 - c) + db * c, da * c + db * (1 - c)

    def slot(da, db):
        dz, dy = zy(da % SIDE, db % SIDE)
        return dz * SIDE + dy

    bar = pltpu.get_barrier_semaphore()
    partners = [(e, right), (e, left), sibling]
    partners += [peer(dz, dy) for dz in range(SIDE) for dy in range(SIDE) if (dz, dy) != (0, 0)]
    for p in partners:
        pl.semaphore_signal(bar, inc=1, device_id=p, device_id_type=MESH)

    wcopies = []
    for g in range(8):
        cols = pl.ds(g * HID, HID)
        wcopies.append(
            pltpu.make_async_copy(w_gate.at[0, :, cols], wgu.at[:, pl.ds(2 * g * HID, HID)], wsem.at[2 * g])
        )
        wcopies.append(
            pltpu.make_async_copy(w_up.at[0, :, cols], wgu.at[:, pl.ds((2 * g + 1) * HID, HID)], wsem.at[2 * g + 1])
        )
    wcopies.append(pltpu.make_async_copy(w_down.at[0], wd, wsem.at[16]))
    for cp in wcopies:
        cp.start()
    pl.semaphore_wait(bar, len(partners))

    sends = []

    def block_at(da, db):
        if (da % SIDE, db % SIDE) == (0, 0):
            return blk
        return gbuf.at[c, slot(da, db)]

    def half_copy(n, da, db, axis, by, half):
        na, nb = (da - by, db) if axis == 0 else (da, db - by)
        ta, tb = (by, 0) if axis == 0 else (0, by)
        dz, dy = zy(ta % SIDE, tb % SIDE)
        return pltpu.make_async_remote_copy(
            src_ref=block_at(da, db).at[HALVES[half]],
            dst_ref=gbuf.at[c, slot(na, nb), HALVES[half]],
            send_sem=gsend.at[n],
            recv_sem=grecv.at[slot(na, nb), half],
            device_id=peer(dz, dy),
            device_id_type=MESH,
        )

    def send_half(*what):
        half_copy(len(sends), *what).start()
        sends.append(what)

    def send_full(da, db, axis):
        for by in (1, -1):
            for half in (0, 1):
                send_half(da, db, axis, by, half)

    sib_copies = []

    def sibling_copy(n, da, db):
        return pltpu.make_async_remote_copy(
            src_ref=block_at(da, db),
            dst_ref=gbuf.at[c, slot(da, db)],
            send_sem=bsend.at[n],
            recv_sem=brecv.at[slot(da, db)],
            device_id=sibling,
            device_id_type=MESH,
        )

    def send_sibling(*what):
        sibling_copy(len(sib_copies), *what).start()
        sib_copies.append(what)

    def wait_half(da, db, half):
        ref = gbuf.at[c, slot(da, db), HALVES[half]]
        pltpu.make_async_copy(ref, ref, grecv.at[slot(da, db), half]).wait()

    def arrived(da, db):
        wait_half(da, db, 0)
        wait_half(da, db, 1)
        if db == 0:
            if da == 3:
                send_half(da, db, 0, 1, 0)
            if da == 1:
                send_half(da, db, 0, -1, 1)
            send_full(da, db, 1)
        elif db == 3:
            send_half(da, db, 1, 1, 0)
        elif db == 1:
            send_half(da, db, 1, -1, 1)
        send_sibling(da, db)

    send_sibling(0, 0)
    send_full(0, 0, 0)
    send_full(0, 0, 1)

    cnt[...] = jnp.zeros_like(cnt)
    for cp in wcopies:
        cp.wait()

    row_i = lax.broadcasted_iota(jnp.int32, (TOK, TOK), 0)
    col_i = lax.broadcasted_iota(jnp.int32, (TOK, TOK), 1)
    upper = (row_i < col_i).astype(BF)
    slot_iota = lax.broadcasted_iota(jnp.int32, (ROWS, TOK), 0).astype(F32)

    def routing(ext, expert, core):
        hit = (ext[0:TOP] == expert).astype(F32)
        mask = jnp.sum(hit, axis=0, keepdims=True)
        scale = jnp.sum(hit * ext[TOP : 2 * TOP], axis=0, keepdims=True)
        rank = dot(jnp.broadcast_to(mask, (16, TOK)).astype(BF), upper, 1, 0)[0:1]
        key = jnp.where(mask > 0.5, rank + float(CAP * core), -1.0)
        return (slot_iota == key).astype(F32), scale

    def remote_x(src, dst, ssem, rsem, to):
        return pltpu.make_async_remote_copy(
            src_ref=src, dst_ref=dst, send_sem=ssem, recv_sem=rsem, device_id=(e, to), device_id_type=MESH
        )

    def rs1(t, h):
        return remote_x(
            part.at[lax.rem(t, 3), 1, h], r1.at[t, h], r1s.at[t, h], r1r.at[t, h], (right, left)[h]
        )

    def rs2(t, side):
        return remote_x(
            part.at[lax.rem(t, 3), 2 * side], r2.at[t, side], r2s.at[t, side], r2r.at[t, side], (right, left)[side]
        )

    def ag1(t, side):
        mine = pl.ds(2 * x, 2)
        return remote_x(
            ag.at[t, mine], ag.at[t, mine], a1s.at[t, side], a1r.at[t, side], (right, left)[side]
        )

    def ag1_wait(t, side):
        ref = ag.at[t, pl.ds(2 * (left, right)[side], 2)]
        pltpu.make_async_copy(ref, ref, a1r.at[t, side]).wait()

    def ag2(t, side):
        ref = ag.at[t, 2 * (left, right)[side] + side]
        return remote_x(ref, ref, a2s.at[t, side], a2r.at[t, side], (right, left)[side])

    def ag2_wait(t, side):
        ref = ag.at[t, 2 * lax.rem(x + 2, SIDE) + side]
        pltpu.make_async_copy(ref, ref, a2r.at[t, side]).wait()

    def ret_copy(k):
        dz, dy = ORDER[k]
        if (dz, dy) == (0, 0):
            return pltpu.make_async_copy(rets.at[k], retr.at[chip], rtr.at[chip])
        return pltpu.make_async_remote_copy(
            src_ref=rets.at[k], dst_ref=retr.at[chip], send_sem=rts.at[k], recv_sem=rtr.at[chip],
            device_id=peer(dz, dy), device_id_type=MESH,
        )

    def forward(s):
        for k in range(CHUNKS):

            @pl.when(s == k)
            def _():
                for ev in EVENTS[k]:
                    arrived(*ev)
                loads = []
                for i in range(GROUP):
                    dz, dy = ORDER[k * GROUP + i]
                    at = dz * SIDE + dy
                    ref = gbuf.at[1 - c, at]
                    pltpu.make_async_copy(ref, ref, brecv.at[at]).wait()
                    mine = blk if at == 0 else gbuf.at[c, at]
                    loads.append(pltpu.make_async_copy(mine, stage.at[i, c], stsem.at[2 * i]))
                    loads.append(pltpu.make_async_copy(ref, stage.at[i, 1 - c], stsem.at[2 * i + 1]))
                for cp in loads:
                    cp.start()
                for cp in loads:
                    cp.wait()

        expert = e.astype(F32)
        for i in range(GROUP):
            picks, scales = [], []
            for core in range(2):
                ext = stage[i, core, pl.ds(2 * TOK, 16), pl.ds(0, 2 * TOK)].astype(F32)
                cnt[...] += ext[:, TOK:]
                pick, scale = routing(ext[:, :TOK], expert, core)
                picks.append(pick)
                scales.append(jnp.sum(pick * scale, axis=1, keepdims=True))
            pick = jnp.concatenate(picks, axis=1).astype(BF)
            rows = pl.ds(pl.multiple_of(s * R + i * ROWS, 16), ROWS)
            scl[s, pl.ds(i * ROWS, ROWS), :] = jnp.broadcast_to(scales[0] + scales[1], (ROWS, HID))
            act = jnp.concatenate([stage[i, 0, pl.ds(0, TOK), :], stage[i, 1, pl.ds(0, TOK), :]], axis=0)
            rowact[pl.ds(i * ROWS, ROWS), :] = dot(pick, act, 1, 0).astype(BF)
            cot = jnp.concatenate([stage[i, 0, pl.ds(TOK, TOK), :], stage[i, 1, pl.ds(TOK, TOK), :]], axis=0)
            rowcot[rows, :] = dot(pick, cot, 1, 0).astype(BF)

        at = lax.rem(s, 3)

        @pl.when(s >= 3)
        def _():
            for h in range(2):
                rs1(s - 3, h).wait_send()
                rs2(s - 3, h).wait_send()

        chunk_rows = pl.ds(pl.multiple_of(s * R, 16), R)
        for j in (2, 1, 3, 0):
            a = lax.rem(x + j, SIDE)
            gu = dot(rowact[...], wgu[:, pl.ds(pl.multiple_of(a * 512, 512), 512)], 1, 0)
            d = dot(rowcot[chunk_rows, :], wd[pl.ds(pl.multiple_of(a * 256, 256), 256), :], 1, 1)
            for h in range(2):
                gu_h = gu[:, 256 * h : 256 * h + 256]
                d_h = d[:, HID * h : HID * h + HID]
                if j == 0:
                    own[at, h, :, pl.ds(0, 256)] = gu_h
                    own[at, h, :, pl.ds(256, HID)] = d_h
                else:
                    part[at, j - 1, h, :, pl.ds(0, 256)] = gu_h.astype(BF)
                    part[at, j - 1, h, :, pl.ds(256, HID)] = d_h.astype(BF)
            if j == 2:
                rs1(s, 0).start()
                rs1(s, 1).start()

    def pass_sums(t):
        at = lax.rem(t, 3)
        for h in range(2):
            rs1(t, h).wait_recv()
            part[at, 2 * h, h] = (part[at, 2 * h, h].astype(F32) + r1[t, h].astype(F32)).astype(BF)
            rs2(t, h).start()

    def pointwise(t):
        at = lax.rem(t, 3)
        rs2(t, 0).wait_recv()
        rs2(t, 1).wait_recv()
        scale = scl[t]
        for h in range(2):
            v = own[at, h] + r2[t, 0, h].astype(F32) + r2[t, 1, h].astype(F32)
            gate, up, down = v[:, :HID], v[:, HID : 2 * HID], v[:, 2 * HID :]
            sig = jax.nn.sigmoid(gate)
            act = gate * sig
            slope = sig * (1.0 + gate * (1.0 - sig))
            dh = down * scale
            g = 2 * x + h
            ag[t, g, :, pl.ds(0, HID)] = (dh * up * slope).astype(BF)
            ag[t, g, :, pl.ds(HID, HID)] = (dh * act).astype(BF)
            ag[t, g, :, pl.ds(2 * HID, HID)] = (act * up * scale).astype(BF)
        ag1(t, 0).start()
        ag1(t, 1).start()

    def pass_shares(t):
        for side in range(2):
            ag1_wait(t, side)
            ag2(t, side).start()

    def backward(t):
        ag2_wait(t, 0)
        ag2_wait(t, 1)
        rows = pl.ds(pl.multiple_of(t * R, 16), R)
        for g in range(8):
            hs[rows, pl.ds(g * HID, HID)] = ag[t, g, :, pl.ds(2 * HID, HID)]
        grads = jnp.concatenate([ag[t, g, :, pl.ds(0, 2 * HID)] for g in range(8)], axis=1)
        out = dot(grads, wgu[...], 1, 1).astype(BF)
        for i in range(GROUP):
            rets[t * GROUP + i] = out[i * ROWS : (i + 1) * ROWS]
        for k in range(CHUNKS):

            @pl.when(t == k)
            def _():
                for i in range(GROUP):
                    ret_copy(k * GROUP + i).start()

    def step(s, carry):
        @pl.when((s >= 1) & (s < CHUNKS + 1))
        def _():
            pass_sums(s - 1)

        @pl.when((s >= 2) & (s < CHUNKS + 2))
        def _():
            pointwise(s - 2)

        @pl.when((s >= 3) & (s < CHUNKS + 3))
        def _():
            pass_shares(s - 3)

        @pl.when(s < CHUNKS)
        def _():
            forward(s)

        @pl.when(s >= 4)
        def _():
            backward(s - 4)

        return carry

    lax.fori_loop(0, CHUNKS + 4, step, 0)

    factor = float(2 * CHIPS * TOK) / cnt[0:1, 0:1]
    outs = []
    for f in range(4):
        if f >= 2:
            outs[f - 2].wait()
        dgt[f % 2] = (dot(hs[:, pl.ds(256 * f, 256)], rowcot[...], 0, 0) * factor).astype(BF)
        cp = pltpu.make_async_copy(dgt.at[f % 2], down_grad.at[0, pl.ds(256 * f, 256), :], osem.at[f % 2])
        cp.start()
        outs.append(cp)

    for core in range(2):
        src = stage.at[0, core, pl.ds(2 * TOK, 16), :]

        @pl.when(c == core)
        def _():
            cp = pltpu.make_async_copy(blk.at[pl.ds(2 * TOK, 16)], src, stsem.at[0])
            cp.start()
            cp.wait()

        @pl.when(c != core)
        def _():
            cp = pltpu.make_async_copy(gbuf.at[1 - c, 0, pl.ds(2 * TOK, 16)], src, stsem.at[0])
            cp.start()
            cp.wait()

    for q in range(CHIPS):
        expert = (2 * q + c).astype(F32)
        for core in range(2):
            ext = stage[0, core, pl.ds(2 * TOK, 16), pl.ds(0, TOK)].astype(F32)
            pick, _ = routing(ext, expert, core)
            sall[pl.ds(q * ROWS, ROWS), pl.ds(core * TOK, TOK)] = pick.astype(BF)
    for dz in range(SIDE):
        for dy in range(SIDE):
            ref = retr.at[chip_at(dz, dy)]
            pltpu.make_async_copy(ref, ref, rtr.at[chip_at(dz, dy)]).wait()
    dense[...] = dot(sall[...], retr[...].reshape(CHIPS * ROWS, width), 0, 0)
    swap = pltpu.make_async_remote_copy(
        src_ref=dense.at[pl.ds(pl.multiple_of((1 - c) * TOK, TOK), TOK)],
        dst_ref=sibr,
        send_sem=css.at[0],
        recv_sem=csr.at[0],
        device_id=sibling,
        device_id_type=MESH,
    )
    swap.start()
    swap.wait()
    mine = dense[pl.ds(pl.multiple_of(c * TOK, TOK), TOK), :]
    igt[...] = ((mine + sibr[...]) * factor).astype(BF)
    final = pltpu.make_async_copy(igt, in_grad, osem.at[2])
    final.start()

    final.wait()
    outs[2].wait()
    outs[3].wait()
    for n, what in enumerate(sends):
        half_copy(n, *what).wait_send()
    for n, what in enumerate(sib_copies):
        sibling_copy(n, *what).wait_send()
    for k in range(1, CHIPS):
        ret_copy(k).wait_send()

    def drain(t, carry):
        for h in range(2):
            @pl.when(t >= CHUNKS - 3)
            def _():
                rs1(t, h).wait_send()
                rs2(t, h).wait_send()

            ag1(t, h).wait_send()
            ag2(t, h).wait_send()
        return carry

    lax.fori_loop(0, CHUNKS, drain, 0)


def local(
    activations, cotangent, expert_ids, combine, log_ratio, valid_mask, segment_ids, w_gate, w_up, w_down
):
    tok_rows, width = activations.shape
    groups = lax.axis_size("expert")
    me = lax.axis_index("expert")
    last = jnp.where(me == groups - 1, -1, segment_ids[-1:])
    following = jnp.concatenate([segment_ids[1:], last])
    live = jnp.maximum(valid_mask, (following != segment_ids).astype(jnp.int32)).astype(F32)
    weight = jnp.minimum(jnp.exp(log_ratio), 2.0) * live
    slot_scale = (combine * weight[:, None]).astype(BF)
    routing = jnp.concatenate([expert_ids.T.astype(BF), slot_scale.T], axis=0)
    count = jnp.broadcast_to(jnp.sum(live).astype(BF), (2 * TOP, TOK))
    ext = jnp.concatenate([routing, count, jnp.zeros((2 * TOP, width - 2 * TOK), BF)], axis=1)
    blk = jnp.concatenate([activations, cotangent, ext], axis=0)

    any_spec = pl.BlockSpec(memory_space=pl.ANY)
    dma = pltpu.SemaphoreType.DMA
    in_grad, down_grad, _ = pl.pallas_call(
        kernel,
        out_shape=(
            jax.ShapeDtypeStruct((tok_rows, width), BF),
            jax.ShapeDtypeStruct(w_down.shape, BF),
            jax.ShapeDtypeStruct((2, CHIPS, BLOCK, width), BF),
        ),
        in_specs=[any_spec] * 4,
        out_specs=(any_spec,) * 3,
        scratch_shapes=[
            pltpu.VMEM((width, 2048), BF),
            pltpu.VMEM((1024, width), BF),
            pltpu.VMEM((GROUP, 2, BLOCK, width), BF),
            pltpu.VMEM((R, width), BF),
            pltpu.VMEM((CHIPS * ROWS, width), BF),
            pltpu.VMEM((CHUNKS, R, HID), F32),
            pltpu.VMEM((3, 3, 2, R, 3 * HID), BF),
            pltpu.VMEM((3, 2, R, 3 * HID), F32),
            pltpu.VMEM((CHUNKS, 2, R, 3 * HID), BF),
            pltpu.VMEM((CHUNKS, 2, 2, R, 3 * HID), BF),
            pltpu.VMEM((CHUNKS, 8, R, 3 * HID), BF),
            pltpu.VMEM((CHIPS * ROWS, 1024), BF),
            pltpu.VMEM((CHIPS, ROWS, width), BF),
            pltpu.VMEM((CHIPS, ROWS, width), BF),
            pltpu.VMEM((2 * TOK, width), F32),
            pltpu.VMEM((TOK, width), F32),
            pltpu.VMEM((CHIPS * ROWS, 2 * TOK), BF),
            pltpu.VMEM((2, 256, width), BF),
            pltpu.VMEM((TOK, width), BF),
            pltpu.VMEM((16, TOK), F32),
            dma((17,)), dma((2 * GROUP,)),
            dma((26 * 2,)), dma((CHIPS, 2)), dma((CHIPS,)), dma((CHIPS,)),
            dma((CHUNKS, 2)), dma((CHUNKS, 2)), dma((CHUNKS, 2)), dma((CHUNKS, 2)),
            dma((CHUNKS, 2)), dma((CHUNKS, 2)), dma((CHUNKS, 2)), dma((CHUNKS, 2)),
            dma((CHIPS,)), dma((CHIPS,)), dma((1,)), dma((1,)), dma((3,)),
        ],
        compiler_params=pltpu.CompilerParams(
            collective_id=0, has_side_effects=True, vmem_limit_bytes=63 * 2**20
        ),
        cost_estimate=pl.CostEstimate(flops=28_200_000_000, bytes_accessed=60_000_000, transcendentals=1_000_000),
    )(blk, w_gate, w_up, w_down)
    return in_grad, down_grad


def solution(mesh):
    return jax.shard_map(
        local,
        mesh=mesh,
        in_specs=(
            P("expert", "tensor"),
            P("expert", "tensor"),
            P("expert", None),
            P("expert", None),
            P("expert"),
            P("expert"),
            P("expert"),
            P("expert", "tensor", None),
            P("expert", "tensor", None),
            P("expert", None, "tensor"),
        ),
        out_specs=(P("expert", "tensor"), P("expert", None, "tensor")),
        check_vma=False,
    )
```

```python
import functools

import jax
import jax.numpy as jnp
from jax import lax
from jax.experimental import pallas as pl
from jax.experimental.pallas import tpu as pltpu
from jax.sharding import PartitionSpec as P

BF = jnp.bfloat16
F32 = jnp.float32
MESH = pl.DeviceIdType.MESH

SIDE = 4
CHIPS = SIDE * SIDE
CAP = 40
TOK = 128
ROWS = 2 * CAP
TOP = 8
HID = 128
LANES = 3 * HID
BLOCK = 2 * TOK + 16
LAST = 8

ORDER = [
    (0, 0),
    (3, 0), (1, 0),
    (0, 3), (0, 1),
    (3, 3), (3, 1),
    (2, 3), (3, 2),
    (2, 2), (2, 1),
    (1, 2), (1, 3),
    (2, 0), (0, 2),
    (1, 1),
]
CHUNK = [ORDER[:1]] + [ORDER[i : i + 2] for i in range(1, 15, 2)] + [ORDER[15:]]
BEFORE = {
    1: [("wait", (3, 0)), ("wait", (1, 0)), ("full", (0, 0), 1)],
    2: [("wait", (0, 3)), ("wait", (0, 1))],
    3: [("wait", (3, 3)), ("wait", (3, 1)), ("half", (3, 3), 1, 1, 0), ("half", (3, 1), 1, -1, 1)],
    4: [
        ("wait", (2, 3)), ("wait", (2, 1)), ("half", (2, 3), 1, 1, 0), ("half", (2, 1), 1, -1, 1),
        ("wait", (3, 2)),
    ],
    5: [("wait", (2, 2))],
    6: [("wait", (1, 2)), ("wait", (0, 2))],
}
AFTER = {
    1: [("half", (3, 0), 0, 1, 0), ("half", (1, 0), 0, -1, 1), ("full", (3, 0), 1)],
    2: [("wait", (2, 0)), ("full", (2, 0), 1)],
    3: [("full", (1, 0), 1)],
    4: [("half", (0, 3), 1, 1, 0), ("half", (0, 1), 1, -1, 1)],
    5: [("wait", (1, 3)), ("wait", (1, 1)), ("half", (1, 3), 1, 1, 0), ("half", (1, 1), 1, -1, 1)],
}
HALVES = (pl.ds(0, TOK), pl.ds(TOK, BLOCK - TOK))


def first_of(t):
    return max(2 * t - 1, 0) if isinstance(t, int) else 2 * t - lax.div(t + 8, 9)


def dot(a, b, ca, cb):
    return lax.dot_general(a, b, (((ca,), (cb,)), ((), ())), preferred_element_type=F32)


def kernel(
    acts, cots, ids, combine, log_ratio, valid, segments, w_gate, w_up, w_down,
    in_grad, down_grad, gbuf,
    wgu, wd, mine, stage, rowact, rowcot, scl, part, own, r1, r2, ag, hs, rets, retr, dense, sibr, sall,
    dgt, igt, cnt,
    wsem, stsem, gsend, grecv, bsend, brecv, r1s, r1r, r2s, r2r, a1s, a1r, a2s, a2r, rts, rtr,
    css, csr, osem,
):
    e = lax.axis_index("expert")
    x = lax.axis_index("tensor")
    c = lax.rem(e, 2)
    chip = lax.div(e, 2)
    z = lax.div(chip, SIDE)
    y = lax.rem(chip, SIDE)
    width = acts.shape[1]
    right = lax.rem(x + 1, SIDE)
    left = lax.rem(x + SIDE - 1, SIDE)

    def chip_at(dz, dy):
        return lax.rem(z + dz, SIDE) * SIDE + lax.rem(y + dy, SIDE)

    def peer(dz, dy):
        return (chip_at(dz, dy) * 2 + c, x)

    sibling = (chip * 2 + 1 - c, x)

    def zy(da, db):
        return da * (1 - c) + db * c, da * c + db * (1 - c)

    def slot(da, db):
        dz, dy = zy(da % SIDE, db % SIDE)
        return dz * SIDE + dy

    bar = pltpu.get_barrier_semaphore()
    partners = [(e, right), (e, left), sibling]
    partners += [peer(dz, dy) for dz in range(SIDE) for dy in range(SIDE) if (dz, dy) != (0, 0)]
    for p in partners:
        pl.semaphore_signal(bar, inc=1, device_id=p, device_id_type=MESH)

    wcopies = []
    for g in range(8):
        cols = pl.ds(g * HID, HID)
        wcopies.append(
            pltpu.make_async_copy(w_gate.at[0, :, cols], wgu.at[:, pl.ds(2 * g * HID, HID)], wsem.at[2 * g])
        )
        wcopies.append(
            pltpu.make_async_copy(w_up.at[0, :, cols], wgu.at[:, pl.ds((2 * g + 1) * HID, HID)], wsem.at[2 * g + 1])
        )
    wcopies.append(pltpu.make_async_copy(w_down.at[0], wd, wsem.at[16]))
    loads = [
        pltpu.make_async_copy(acts, mine.at[pl.ds(0, TOK)], stsem.at[0]),
        pltpu.make_async_copy(cots, mine.at[pl.ds(TOK, TOK)], stsem.at[1]),
    ]
    for cp in loads + wcopies:
        cp.start()

    lane = lax.broadcasted_iota(jnp.int32, (TOP, TOK), 1)
    seg = jnp.broadcast_to(segments[...], (TOP, TOK))
    following = pltpu.roll(seg, TOK - 1, 1)
    final_dev = (e + 1) // (2 * CHIPS)
    closing = jnp.where(lane == TOK - 1, final_dev, (following != seg).astype(jnp.int32))
    live = jnp.maximum(jnp.broadcast_to(valid[...], (TOP, TOK)), closing).astype(F32)
    weight = jnp.minimum(jnp.exp(jnp.broadcast_to(log_ratio[...], (TOP, TOK))), 2.0) * live
    slot_scale = (combine[...].T * weight).astype(BF)
    count = jnp.broadcast_to(jnp.sum(live, axis=1, keepdims=True), (TOP, TOK)).astype(BF)
    tail = pl.ds(2 * TOK, 2 * TOP)
    mine[tail, :] = jnp.zeros((2 * TOP, width), BF)
    mine[tail, pl.ds(0, TOK)] = jnp.concatenate([ids[...].astype(F32).T.astype(BF), slot_scale], axis=0)
    mine[tail, pl.ds(TOK, TOK)] = jnp.concatenate([count, count], axis=0)
    for cp in loads:
        cp.wait()
    pl.semaphore_wait(bar, len(partners))

    sends = []

    def block_at(da, db):
        if (da % SIDE, db % SIDE) == (0, 0):
            return mine
        return gbuf.at[c, slot(da, db)]

    def half_copy(n, da, db, axis, by, half):
        na, nb = (da - by, db) if axis == 0 else (da, db - by)
        ta, tb = (by, 0) if axis == 0 else (0, by)
        dz, dy = zy(ta % SIDE, tb % SIDE)
        return pltpu.make_async_remote_copy(
            src_ref=block_at(da, db).at[HALVES[half]],
            dst_ref=gbuf.at[c, slot(na, nb), HALVES[half]],
            send_sem=gsend.at[n],
            recv_sem=grecv.at[slot(na, nb), half],
            device_id=peer(dz, dy),
            device_id_type=MESH,
        )

    def send_half(*what):
        half_copy(len(sends), *what).start()
        sends.append(what)

    def send_full(da, db, axis):
        for by in (1, -1):
            for half in (0, 1):
                send_half(da, db, axis, by, half)

    sib_copies = []

    def sibling_copy(n, da, db):
        return pltpu.make_async_remote_copy(
            src_ref=block_at(da, db),
            dst_ref=gbuf.at[c, slot(da, db)],
            send_sem=bsend.at[n],
            recv_sem=brecv.at[slot(da, db)],
            device_id=sibling,
            device_id_type=MESH,
        )

    def send_sibling(*what):
        sibling_copy(len(sib_copies), *what).start()
        sib_copies.append(what)

    def wait_half(da, db, half):
        ref = gbuf.at[c, slot(da, db), HALVES[half]]
        pltpu.make_async_copy(ref, ref, grecv.at[slot(da, db), half]).wait()

    def act_on(events):
        for kind, at, *rest in events:
            if kind == "wait":
                wait_half(*at, 0)
                wait_half(*at, 1)
                send_sibling(*at)
            elif kind == "full":
                send_full(*at, *rest)
            else:
                send_half(*at, *rest)

    send_sibling(0, 0)
    send_full(0, 0, 0)

    cnt[...] = jnp.zeros_like(cnt)

    row_i = lax.broadcasted_iota(jnp.int32, (TOK, TOK), 0)
    col_i = lax.broadcasted_iota(jnp.int32, (TOK, TOK), 1)
    upper = (row_i < col_i).astype(BF)
    slot_iota = lax.broadcasted_iota(jnp.int32, (ROWS, TOK), 0).astype(F32)

    def routing(ext, expert, core):
        hit = (ext[0:TOP] == expert).astype(F32)
        mask = jnp.sum(hit, axis=0, keepdims=True)
        scale = jnp.sum(hit * ext[TOP : 2 * TOP], axis=0, keepdims=True)
        rank = dot(jnp.broadcast_to(mask, (16, TOK)).astype(BF), upper, 1, 0)[0:1]
        key = jnp.where(mask > 0.5, rank + float(CAP * core), -1.0)
        return (slot_iota == key).astype(F32), scale

    def remote_x(src, dst, ssem, rsem, to):
        return pltpu.make_async_remote_copy(
            src_ref=src, dst_ref=dst, send_sem=ssem, recv_sem=rsem, device_id=(e, to), device_id_type=MESH
        )

    def rs1(t, n, h):
        return remote_x(
            part.at[lax.rem(t, 3), pl.ds(0, n), 1, h], r1.at[pl.ds(first_of(t), n), h],
            r1s.at[t, h], r1r.at[t, h], (right, left)[h],
        )

    def rs2(t, n, side):
        return remote_x(
            part.at[lax.rem(t, 3), pl.ds(0, n), 2 * side], r2.at[pl.ds(first_of(t), n), side],
            r2s.at[t, side], r2r.at[t, side], (right, left)[side],
        )

    def ag1(t, n, side):
        ref = ag.at[pl.ds(first_of(t), n), pl.ds(2 * x, 2)]
        return remote_x(ref, ref, a1s.at[t, side], a1r.at[t, side], (right, left)[side])

    def ag1_wait(t, n, side):
        ref = ag.at[pl.ds(first_of(t), n), pl.ds(2 * (left, right)[side], 2)]
        pltpu.make_async_copy(ref, ref, a1r.at[t, side]).wait()

    def ag2(t, n, side):
        ref = ag.at[pl.ds(first_of(t), n), 2 * (left, right)[side] + side]
        return remote_x(ref, ref, a2s.at[t, side], a2r.at[t, side], (right, left)[side])

    def ag2_wait(t, n, side):
        ref = ag.at[pl.ds(first_of(t), n), 2 * lax.rem(x + 2, SIDE) + side]
        pltpu.make_async_copy(ref, ref, a2r.at[t, side]).wait()

    def ret_copy(k):
        dz, dy = ORDER[k]
        if k == 0:
            return pltpu.make_async_copy(rets.at[0], retr.at[0], rtr.at[0])
        return pltpu.make_async_remote_copy(
            src_ref=rets.at[k], dst_ref=retr.at[k], send_sem=rts.at[k], recv_sem=rtr.at[k],
            device_id=peer(dz, dy), device_id_type=MESH,
        )

    def load_stage(elements):
        copies = []
        for i, at in enumerate(elements):
            da, db = at
            theirs = (da * c + db * (1 - c)) * SIDE + da * (1 - c) + db * c
            ref = gbuf.at[1 - c, theirs]
            pltpu.make_async_copy(ref, ref, brecv.at[theirs]).wait()
            copies.append(pltpu.make_async_copy(block_at(*at), stage.at[i, c], stsem.at[2 * i]))
            copies.append(pltpu.make_async_copy(ref, stage.at[i, 1 - c], stsem.at[2 * i + 1]))
        for cp in copies:
            cp.start()
        for cp in copies:
            cp.wait()

    def sends_done(t, n):
        for h in range(2):
            rs1(t, n, h).wait_send()
            rs2(t, n, h).wait_send()

    def forward(t, n):
        first = first_of(t)
        expert = e.astype(F32)
        for i in range(n):
            picks, scales = [], []
            for core in range(2):
                ext = stage[i, core, pl.ds(2 * TOK, 16), pl.ds(0, 2 * TOK)].astype(F32)
                cnt[...] += ext[:, TOK:]
                pick, scale = routing(ext[:, :TOK], expert, core)
                picks.append(pick)
                scales.append(jnp.sum(pick * scale, axis=1, keepdims=True))
            pick = jnp.concatenate(picks, axis=1).astype(BF)
            rows = pl.ds(pl.multiple_of((first + i) * ROWS, 16), ROWS)
            scl[first + i] = jnp.broadcast_to(scales[0] + scales[1], (ROWS, HID))
            act = jnp.concatenate([stage[i, 0, pl.ds(0, TOK), :], stage[i, 1, pl.ds(0, TOK), :]], axis=0)
            rowact[pl.ds(i * ROWS, ROWS), :] = dot(pick, act, 1, 0).astype(BF)
            cot = jnp.concatenate([stage[i, 0, pl.ds(TOK, TOK), :], stage[i, 1, pl.ds(TOK, TOK), :]], axis=0)
            rowcot[rows, :] = dot(pick, cot, 1, 0).astype(BF)

        at = lax.rem(t, 3)
        chunk_rows = pl.ds(pl.multiple_of(first * ROWS, 16), n * ROWS)
        for j in (2, 1, 3, 0):
            a = lax.rem(x + j, SIDE)
            gu = dot(rowact[pl.ds(0, n * ROWS), :], wgu[:, pl.ds(pl.multiple_of(a * 512, 512), 512)], 1, 0)
            d = dot(rowcot[chunk_rows, :], wd[pl.ds(pl.multiple_of(a * 256, 256), 256), :], 1, 1)
            for i in range(n):
                for h in range(2):
                    gu_h = gu[i * ROWS : (i + 1) * ROWS, 256 * h : 256 * h + 256]
                    d_h = d[i * ROWS : (i + 1) * ROWS, HID * h : HID * h + HID]
                    if j == 0:
                        own[at, i, h, :, pl.ds(0, 256)] = gu_h
                        own[at, i, h, :, pl.ds(256, HID)] = d_h
                    else:
                        part[at, i, j - 1, h, :, pl.ds(0, 256)] = gu_h.astype(BF)
                        part[at, i, j - 1, h, :, pl.ds(256, HID)] = d_h.astype(BF)
            if j == 2:
                rs1(t, n, 0).start()
                rs1(t, n, 1).start()

    def pass_sums(t, n):
        at = lax.rem(t, 3)
        first = first_of(t)
        for h in range(2):
            rs1(t, n, h).wait_recv()
            for i in range(n):
                part[at, i, 2 * h, h] = (part[at, i, 2 * h, h].astype(F32) + r1[first + i, h].astype(F32)).astype(BF)
            rs2(t, n, h).start()

    def pointwise(t, n):
        at = lax.rem(t, 3)
        first = first_of(t)
        rs2(t, n, 0).wait_recv()
        rs2(t, n, 1).wait_recv()
        for i in range(n):
            scale = scl[first + i]
            for h in range(2):
                v = own[at, i, h] + r2[first + i, 0, h].astype(F32) + r2[first + i, 1, h].astype(F32)
                gate, up, down = v[:, :HID], v[:, HID : 2 * HID], v[:, 2 * HID :]
                sig = jax.nn.sigmoid(gate)
                act = gate * sig
                slope = sig * (1.0 + gate * (1.0 - sig))
                dh = down * scale
                g = 2 * x + h
                ag[first + i, g, :, pl.ds(0, HID)] = (dh * up * slope).astype(BF)
                ag[first + i, g, :, pl.ds(HID, HID)] = (dh * act).astype(BF)
                ag[first + i, g, :, pl.ds(2 * HID, HID)] = (act * up * scale).astype(BF)
        ag1(t, n, 0).start()
        ag1(t, n, 1).start()

    def pass_shares(t, n):
        for side in range(2):
            ag1_wait(t, n, side)
            ag2(t, n, side).start()

    def backward(t, n):
        ag2_wait(t, n, 0)
        ag2_wait(t, n, 1)
        first = first_of(t)
        grads = []
        for i in range(n):
            rows = pl.ds(pl.multiple_of((first + i) * ROWS, 16), ROWS)
            for g in range(8):
                hs[rows, pl.ds(g * HID, HID)] = ag[first + i, g, :, pl.ds(2 * HID, HID)]
            grads.append(jnp.concatenate([ag[first + i, g, :, pl.ds(0, 2 * HID)] for g in range(8)], axis=1))
        grads = jnp.concatenate(grads, axis=0) if n > 1 else grads[0]
        rowact[pl.ds(0, n * ROWS), :] = dot(grads, wgu[...], 1, 1).astype(BF)

        core0 = lax.broadcasted_iota(jnp.int32, (ROWS, width), 0) < CAP
        for k, elements in enumerate(CHUNK):
            if len(elements) != n:
                continue

            @pl.when(t == k)
            def _():
                for i, (da, db) in enumerate(elements):
                    k0, k1 = ORDER.index((da, db)), ORDER.index((db, da))
                    out = rowact[pl.ds(i * ROWS, ROWS), :]
                    if k0 < k1:
                        rets[k0] = out
                        rets[k1] = out
                    elif k0 == k1:
                        rets[k0] = out
                        ret_copy(k0).start()
                    else:
                        wide = out.astype(F32)
                        rets[k0] = jnp.where(core0, wide, rets[k0].astype(F32)).astype(BF)
                        rets[k1] = jnp.where(core0, rets[k1].astype(F32), wide).astype(BF)
                        ret_copy(k0).start()
                        ret_copy(k1).start()

    def on(cond, f, *args):
        @pl.when(cond)
        def _():
            f(*args)

    def any_size(t, f):
        on((t >= 1) & (t < LAST), f, t, 2)
        on(t == LAST, f, t, 1)

    load_stage(CHUNK[0])
    for cp in wcopies:
        cp.wait()
    forward(0, 1)
    for core in range(2):
        ext = stage[0, core, pl.ds(2 * TOK, 16), pl.ds(0, TOK)].astype(F32)
        for k, (dz, dy) in enumerate(ORDER):
            expert = (2 * chip_at(-dz % SIDE, -dy % SIDE) + c).astype(F32)
            pick, _ = routing(ext, expert, core)
            sall[pl.ds(k * ROWS, ROWS), pl.ds(core * TOK, TOK)] = pick.astype(BF)
    pass_sums(0, 1)
    pointwise(0, 1)

    def step(s, carry):
        any_size(s - 1, pass_sums)
        any_size(s - 2, pointwise)
        for k in range(1, LAST + 1):

            @pl.when(s == k)
            def _():
                act_on(BEFORE.get(k, []))
                load_stage(CHUNK[k])

        on(s == 3, sends_done, 0, 1)
        on((s >= 4) & (s <= LAST), sends_done, s - 3, 2)
        any_size(s, forward)
        for k in AFTER:

            @pl.when(s == k)
            def _():
                act_on(AFTER[k])

        on(s == 1, pass_shares, 0, 1)
        any_size(s - 2, pass_shares)
        t = s - 3
        on((t >= 1) & (t < LAST), backward, t, 2)
        on((t == 0) | (t == LAST), backward, t, 1)
        return carry

    lax.fori_loop(1, LAST + 4, step, 0)

    factor = float(2 * CHIPS * TOK) / cnt[0:1, 0:1]
    outs = []
    for f in range(4):
        if f >= 2:
            outs[f - 2].wait()
        dgt[f % 2] = (dot(hs[:, pl.ds(256 * f, 256)], rowcot[...], 0, 0) * factor).astype(BF)
        cp = pltpu.make_async_copy(dgt.at[f % 2], down_grad.at[0, pl.ds(256 * f, 256), :], osem.at[f % 2])
        cp.start()
        outs.append(cp)

    for k in range(CHIPS):
        pltpu.make_async_copy(retr.at[k], retr.at[k], rtr.at[k]).wait()
    dense[...] = dot(sall[...], retr[...].reshape(CHIPS * ROWS, width), 0, 0)
    swap = pltpu.make_async_remote_copy(
        src_ref=dense.at[pl.ds(pl.multiple_of((1 - c) * TOK, TOK), TOK)],
        dst_ref=sibr,
        send_sem=css.at[0],
        recv_sem=csr.at[0],
        device_id=sibling,
        device_id_type=MESH,
    )
    swap.start()
    swap.wait()
    kept = dense[pl.ds(pl.multiple_of(c * TOK, TOK), TOK), :]
    igt[...] = ((kept + sibr[...]) * factor).astype(BF)
    final = pltpu.make_async_copy(igt, in_grad, osem.at[2])
    final.start()

    final.wait()
    outs[2].wait()
    outs[3].wait()
    for n, what in enumerate(sends):
        half_copy(n, *what).wait_send()
    for n, what in enumerate(sib_copies):
        sibling_copy(n, *what).wait_send()
    for k in range(1, CHIPS):
        ret_copy(k).wait_send()

    for t in (6, 7):
        sends_done(t, 2)
    sends_done(LAST, 1)

    def drain(t, n):
        for h in range(2):
            ag1(t, n, h).wait_send()
            ag2(t, n, h).wait_send()

    def drain_pair(t, carry):
        drain(t, 2)
        return carry

    drain(0, 1)
    lax.fori_loop(1, LAST, drain_pair, 0)
    drain(LAST, 1)


def local(
    activations, cotangent, expert_ids, combine, log_ratio, valid_mask, segment_ids, w_gate, w_up, w_down
):
    tok_rows, width = activations.shape
    any_spec = pl.BlockSpec(memory_space=pl.ANY)
    dma = pltpu.SemaphoreType.DMA
    in_grad, down_grad, _ = pl.pallas_call(
        kernel,
        out_shape=(
            jax.ShapeDtypeStruct((tok_rows, width), BF),
            jax.ShapeDtypeStruct(w_down.shape, BF),
            jax.ShapeDtypeStruct((2, CHIPS, BLOCK, width), BF),
        ),
        in_specs=[any_spec] * 2 + [pl.BlockSpec(memory_space=pltpu.VMEM)] * 5 + [any_spec] * 3,
        out_specs=(any_spec,) * 3,
        scratch_shapes=[
            pltpu.VMEM((width, 2048), BF),
            pltpu.VMEM((1024, width), BF),
            pltpu.VMEM((BLOCK, width), BF),
            pltpu.VMEM((2, 2, BLOCK, width), BF),
            pltpu.VMEM((2 * ROWS, width), BF),
            pltpu.VMEM((CHIPS * ROWS, width), BF),
            pltpu.VMEM((CHIPS, ROWS, HID), F32),
            pltpu.VMEM((3, 2, 3, 2, ROWS, LANES), BF),
            pltpu.VMEM((3, 2, 2, ROWS, LANES), F32),
            pltpu.VMEM((CHIPS, 2, ROWS, LANES), BF),
            pltpu.VMEM((CHIPS, 2, 2, ROWS, LANES), BF),
            pltpu.VMEM((CHIPS, 8, ROWS, LANES), BF),
            pltpu.VMEM((CHIPS * ROWS, 1024), BF),
            pltpu.VMEM((CHIPS, ROWS, width), BF),
            pltpu.VMEM((CHIPS, ROWS, width), BF),
            pltpu.VMEM((2 * TOK, width), F32),
            pltpu.VMEM((TOK, width), F32),
            pltpu.VMEM((CHIPS * ROWS, 2 * TOK), BF),
            pltpu.VMEM((2, 256, width), BF),
            pltpu.VMEM((TOK, width), BF),
            pltpu.VMEM((16, TOK), F32),
            dma((17,)), dma((4,)),
            dma((26 * 2,)), dma((CHIPS, 2)), dma((CHIPS,)), dma((CHIPS,)),
            dma((LAST + 1, 2)), dma((LAST + 1, 2)), dma((LAST + 1, 2)), dma((LAST + 1, 2)),
            dma((LAST + 1, 2)), dma((LAST + 1, 2)), dma((LAST + 1, 2)), dma((LAST + 1, 2)),
            dma((CHIPS,)), dma((CHIPS,)), dma((1,)), dma((1,)), dma((3,)),
        ],
        compiler_params=pltpu.CompilerParams(
            collective_id=0, has_side_effects=True, vmem_limit_bytes=63 * 2**20
        ),
        cost_estimate=pl.CostEstimate(flops=28_200_000_000, bytes_accessed=60_000_000, transcendentals=1_000_000),
    )(
        activations, cotangent, expert_ids, combine, log_ratio[None], valid_mask[None], segment_ids[None],
        w_gate, w_up, w_down,
    )
    return in_grad, down_grad


def solution(mesh):
    return jax.shard_map(
        local,
        mesh=mesh,
        in_specs=(
            P("expert", "tensor"),
            P("expert", "tensor"),
            P("expert", None),
            P("expert", None),
            P("expert"),
            P("expert"),
            P("expert"),
            P("expert", "tensor", None),
            P("expert", "tensor", None),
            P("expert", None, "tensor"),
        ),
        out_specs=(P("expert", "tensor"), P("expert", None, "tensor")),
        check_vma=False,
    )
```

```python
import functools

import jax
import jax.numpy as jnp
from jax import lax
from jax.experimental import pallas as pl
from jax.experimental.pallas import tpu as pltpu
from jax.sharding import PartitionSpec as P

BF = jnp.bfloat16
F32 = jnp.float32
MESH = pl.DeviceIdType.MESH

SIDE = 4
CHIPS = SIDE * SIDE
CAP = 40
TOK = 128
ROWS = 2 * CAP
TOP = 8
HID = 128
LANES = 3 * HID
BLOCK = 2 * TOK
LAST = 8

ORDER = [
    (0, 0),
    (1, 0), (3, 0),
    (0, 1), (0, 3),
    (1, 3), (1, 1),
    (3, 3), (3, 1),
    (2, 1), (1, 2),
    (3, 2), (2, 3),
    (2, 0), (0, 2),
    (2, 2),
]
CHUNK = [ORDER[:1]] + [ORDER[i : i + 2] for i in range(1, 15, 2)] + [ORDER[15:]]
PASS_ON = {
    (0, "S"): [
        ("full", (0, 0), 1),
    ],
    (0, "P"): [
        ("wait", (3, 0)),
        ("wait", (1, 0)),
    ],
    (1, "L"): [
        ("full", (1, 0), 1),
    ],
    (1, "F"): [
        ("wait", (0, 1)),
        ("half", (3, 0), 0, 1, 0),
        ("wait", (0, 3)),
    ],
    (2, "L"): [
        ("full", (3, 0), 1),
    ],
    (3, "P"): [
        ("wait", (1, 1)),
        ("wait", (1, 3)),
        ("half", (1, 0), 0, -1, 1),
    ],
    (3, "B"): [
        ("half", (1, 1), 1, -1, 1),
    ],
    (3, "L"): [
        ("half", (1, 3), 1, 1, 0),
    ],
    (3, "F"): [
        ("wait", (3, 3)),
    ],
    (4, "P"): [
        ("half", (0, 1), 1, -1, 1),
        ("wait", (3, 1)),
        ("wait", (2, 0)),
    ],
    (4, "S"): [
        ("half", (0, 3), 1, 1, 0),
        ("full", (2, 0), 1),
    ],
    (4, "L"): [
        ("half", (3, 1), 1, -1, 1),
    ],
    (4, "F"): [
        ("wait", (1, 2)),
    ],
    (4, "H"): [
        ("half", (3, 3), 1, 1, 0),
    ],
    (5, "P"): [
        ("wait", (2, 1)),
    ],
    (5, "B"): [
        ("wait", (3, 2)),
    ],
    (5, "L"): [
        ("half", (2, 1), 1, -1, 1),
    ],
    (5, "F"): [
        ("wait", (2, 3)),
    ],
    (6, "F"): [
        ("half", (2, 3), 1, 1, 0),
    ],
    (7, "P"): [
        ("wait", (2, 2)),
        ("wait", (0, 2)),
    ],
}
HALVES = (pl.ds(0, TOK), pl.ds(TOK, BLOCK - TOK))


def first_of(t):
    return max(2 * t - 1, 0) if isinstance(t, int) else 2 * t - lax.div(t + 8, 9)


def dot(a, b, ca, cb):
    return lax.dot_general(a, b, (((ca,), (cb,)), ((), ())), preferred_element_type=F32)


def kernel(
    acts, cots, ids, combine, log_ratio, valid, segments, w_gate, w_up, w_down,
    in_grad, down_grad, gbuf,
    wgu, wd, mine, gext, ext_now, stage, rowact, rowcot, scl, part, own, r1, r2, ag, hs, rets, retr, dense, sibr, sall,
    dgt, igt,
    wsem, stsem, xsend, xrecv, gsend, grecv, bsend, brecv, r1s, r1r, r2s, r2r, a1s, a1r, a2s, a2r, rts, rtr,
    css, csr, osem,
):
    e = lax.axis_index("expert")
    x = lax.axis_index("tensor")
    c = lax.rem(e, 2)
    chip = lax.div(e, 2)
    z = lax.div(chip, SIDE)
    y = lax.rem(chip, SIDE)
    width = acts.shape[1]
    right = lax.rem(x + 1, SIDE)
    left = lax.rem(x + SIDE - 1, SIDE)

    def chip_at(dz, dy):
        return lax.rem(z + dz, SIDE) * SIDE + lax.rem(y + dy, SIDE)

    def peer(dz, dy):
        return (chip_at(dz, dy) * 2 + c, x)

    sibling = (chip * 2 + 1 - c, x)

    def zy(da, db):
        return da * (1 - c) + db * c, da * c + db * (1 - c)

    def slot(da, db):
        dz, dy = zy(da % SIDE, db % SIDE)
        return dz * SIDE + dy

    bar = pltpu.get_barrier_semaphore()
    partners = [(e, right), (e, left), sibling]
    partners += [peer(dz, dy) for dz in range(SIDE) for dy in range(SIDE) if (dz, dy) != (0, 0)]
    for p in partners:
        pl.semaphore_signal(bar, inc=1, device_id=p, device_id_type=MESH)

    wcopies = []
    for g in range(8):
        cols = pl.ds(g * HID, HID)
        wcopies.append(
            pltpu.make_async_copy(w_gate.at[0, :, cols], wgu.at[:, pl.ds(2 * g * HID, HID)], wsem.at[2 * g])
        )
        wcopies.append(
            pltpu.make_async_copy(w_up.at[0, :, cols], wgu.at[:, pl.ds((2 * g + 1) * HID, HID)], wsem.at[2 * g + 1])
        )
    wcopies.append(pltpu.make_async_copy(w_down.at[0], wd, wsem.at[16]))
    loads = [
        pltpu.make_async_copy(acts, mine.at[pl.ds(0, TOK)], stsem.at[0]),
        pltpu.make_async_copy(cots, mine.at[pl.ds(TOK, TOK)], stsem.at[1]),
    ]
    for cp in loads + wcopies:
        cp.start()

    lane = lax.broadcasted_iota(jnp.int32, (TOP, TOK), 1)
    seg = jnp.broadcast_to(segments[...], (TOP, TOK))
    following = pltpu.roll(seg, TOK - 1, 1)
    final_dev = (e + 1) // (2 * CHIPS)
    closing = jnp.where(lane == TOK - 1, final_dev, (following != seg).astype(jnp.int32))
    live = jnp.maximum(jnp.broadcast_to(valid[...], (TOP, TOK)), closing).astype(F32)
    weight = jnp.minimum(jnp.exp(jnp.broadcast_to(log_ratio[...], (TOP, TOK))), 2.0) * live
    slot_scale = (combine[...] * weight).astype(BF)
    count = jnp.broadcast_to(jnp.sum(live, axis=1, keepdims=True), (TOP, TOK)).astype(BF)
    ids_scales = jnp.concatenate([ids[...].astype(F32).astype(BF), slot_scale], axis=0)
    gext[c, 0, :, pl.ds(0, TOK)] = ids_scales
    gext[c, 0, :, pl.ds(TOK, TOK)] = jnp.concatenate([count, count], axis=0)
    for cp in loads:
        cp.wait()
    pl.semaphore_wait(bar, len(partners))

    sends = []

    def block_at(da, db):
        if (da % SIDE, db % SIDE) == (0, 0):
            return mine
        return gbuf.at[c, slot(da, db)]

    def half_copy(n, da, db, axis, by, half):
        na, nb = (da - by, db) if axis == 0 else (da, db - by)
        ta, tb = (by, 0) if axis == 0 else (0, by)
        dz, dy = zy(ta % SIDE, tb % SIDE)
        return pltpu.make_async_remote_copy(
            src_ref=block_at(da, db).at[HALVES[half]],
            dst_ref=gbuf.at[c, slot(na, nb), HALVES[half]],
            send_sem=gsend.at[n],
            recv_sem=grecv.at[slot(na, nb), half],
            device_id=peer(dz, dy),
            device_id_type=MESH,
        )

    def send_half(*what):
        half_copy(len(sends), *what).start()
        sends.append(what)

    def send_full(da, db, axis):
        for by in (1, -1):
            for half in (0, 1):
                send_half(da, db, axis, by, half)

    sib_copies = []

    def sibling_copy(n, da, db):
        return pltpu.make_async_remote_copy(
            src_ref=block_at(da, db),
            dst_ref=gbuf.at[c, slot(da, db)],
            send_sem=bsend.at[n],
            recv_sem=brecv.at[slot(da, db)],
            device_id=sibling,
            device_id_type=MESH,
        )

    def send_sibling(*what):
        sibling_copy(len(sib_copies), *what).start()
        sib_copies.append(what)

    def wait_half(da, db, half):
        ref = gbuf.at[c, slot(da, db), HALVES[half]]
        pltpu.make_async_copy(ref, ref, grecv.at[slot(da, db), half]).wait()

    def act_on(events):
        for kind, at, *rest in events:
            if kind == "wait":
                wait_half(*at, 0)
                wait_half(*at, 1)
                send_sibling(*at)
            elif kind == "full":
                send_full(*at, *rest)
            else:
                send_half(*at, *rest)

    def ext_copy(dz, dy):
        n = dz * SIDE + dy
        to = (-dz % SIDE) * SIDE + -dy % SIDE
        return pltpu.make_async_remote_copy(
            src_ref=gext.at[c, 0], dst_ref=gext.at[c, to], send_sem=xsend.at[n], recv_sem=xrecv.at[to],
            device_id=sibling if n == 0 else peer(dz, dy), device_id_type=MESH,
        )

    def ext_relay():
        others = gext.at[c, pl.ds(1, CHIPS - 1)]
        return pltpu.make_async_remote_copy(
            src_ref=others, dst_ref=others, send_sem=xsend.at[CHIPS], recv_sem=xrecv.at[CHIPS],
            device_id=sibling, device_id_type=MESH,
        )

    offsets = [(dz, dy) for dz in range(SIDE) for dy in range(SIDE)]
    ext_copy(0, 0).start()
    send_sibling(0, 0)
    for at in offsets[1:]:
        ext_copy(*at).start()
    send_full(0, 0, 0)

    row_i = lax.broadcasted_iota(jnp.int32, (TOK, TOK), 0)
    col_i = lax.broadcasted_iota(jnp.int32, (TOK, TOK), 1)
    upper = (row_i < col_i).astype(BF)
    slot_iota = lax.broadcasted_iota(jnp.int32, (ROWS, TOK), 0).astype(F32)

    def routing(ext, expert, core):
        hit = (ext[0:TOP] == expert).astype(F32)
        mask = jnp.sum(hit, axis=0, keepdims=True)
        scale = jnp.sum(hit * ext[TOP : 2 * TOP], axis=0, keepdims=True)
        rank = dot(jnp.broadcast_to(mask, (16, TOK)).astype(BF), upper, 1, 0)[0:1]
        key = jnp.where(mask > 0.5, rank + float(CAP * core), -1.0)
        return (slot_iota == key).astype(F32), scale

    def remote_x(src, dst, ssem, rsem, to):
        return pltpu.make_async_remote_copy(
            src_ref=src, dst_ref=dst, send_sem=ssem, recv_sem=rsem, device_id=(e, to), device_id_type=MESH
        )

    def rs1(t, n, h):
        return remote_x(
            part.at[lax.rem(t, 3), pl.ds(0, n), 1, h], r1.at[pl.ds(first_of(t), n), h],
            r1s.at[t, h], r1r.at[t, h], (right, left)[h],
        )

    def rs2(t, n, side):
        return remote_x(
            part.at[lax.rem(t, 3), pl.ds(0, n), 2 * side], r2.at[pl.ds(first_of(t), n), side],
            r2s.at[t, side], r2r.at[t, side], (right, left)[side],
        )

    def ag1(t, n, side):
        ref = ag.at[pl.ds(first_of(t), n), pl.ds(2 * x, 2)]
        return remote_x(ref, ref, a1s.at[t, side], a1r.at[t, side], (right, left)[side])

    def ag1_wait(t, n, side):
        ref = ag.at[pl.ds(first_of(t), n), pl.ds(2 * (left, right)[side], 2)]
        pltpu.make_async_copy(ref, ref, a1r.at[t, side]).wait()

    def ag2(t, n, side):
        ref = ag.at[pl.ds(first_of(t), n), 2 * (left, right)[side] + side]
        return remote_x(ref, ref, a2s.at[t, side], a2r.at[t, side], (right, left)[side])

    def ag2_wait(t, n, side):
        ref = ag.at[pl.ds(first_of(t), n), 2 * lax.rem(x + 2, SIDE) + side]
        pltpu.make_async_copy(ref, ref, a2r.at[t, side]).wait()

    def ret_copy(k):
        dz, dy = ORDER[k]
        if k == 0:
            return pltpu.make_async_copy(rets.at[0], retr.at[0], rtr.at[0])
        return pltpu.make_async_remote_copy(
            src_ref=rets.at[k], dst_ref=retr.at[k], send_sem=rts.at[k], recv_sem=rtr.at[k],
            device_id=peer(dz, dy), device_id_type=MESH,
        )

    def load_stage(elements):
        copies = []
        for i, at in enumerate(elements):
            da, db = at
            if at != (0, 0):
                ext_now[i, 0] = gext[0, da * SIDE + db, :, pl.ds(0, TOK)]
                ext_now[i, 1] = gext[1, db * SIDE + da, :, pl.ds(0, TOK)]
            theirs = (da * c + db * (1 - c)) * SIDE + da * (1 - c) + db * c
            ref = gbuf.at[1 - c, theirs]
            pltpu.make_async_copy(ref, ref, brecv.at[theirs]).wait()
            copies.append(pltpu.make_async_copy(block_at(*at), stage.at[i, c], stsem.at[2 * i]))
            copies.append(pltpu.make_async_copy(ref, stage.at[i, 1 - c], stsem.at[2 * i + 1]))
        for cp in copies:
            cp.start()
        for cp in copies:
            cp.wait()

    def sends_done(t, n):
        for h in range(2):
            rs1(t, n, h).wait_send()
            rs2(t, n, h).wait_send()

    def forward(t, n):
        first = first_of(t)
        expert = e.astype(F32)
        for i in range(n):
            picks, scales = [], []
            for core in range(2):
                pick, scale = routing(ext_now[i, core].astype(F32), expert, core)
                picks.append(pick)
                scales.append(jnp.sum(pick * scale, axis=1, keepdims=True))
            pick = jnp.concatenate(picks, axis=1).astype(BF)
            rows = pl.ds(pl.multiple_of((first + i) * ROWS, 16), ROWS)
            scl[first + i] = jnp.broadcast_to(scales[0] + scales[1], (ROWS, HID))
            act = jnp.concatenate([stage[i, 0, pl.ds(0, TOK), :], stage[i, 1, pl.ds(0, TOK), :]], axis=0)
            rowact[pl.ds(i * ROWS, ROWS), :] = dot(pick, act, 1, 0).astype(BF)
            cot = jnp.concatenate([stage[i, 0, pl.ds(TOK, TOK), :], stage[i, 1, pl.ds(TOK, TOK), :]], axis=0)
            rowcot[rows, :] = dot(pick, cot, 1, 0).astype(BF)

        at = lax.rem(t, 3)
        chunk_rows = pl.ds(pl.multiple_of(first * ROWS, 16), n * ROWS)
        for j in (2, 1, 3, 0):
            a = lax.rem(x + j, SIDE)
            gu = dot(rowact[pl.ds(0, n * ROWS), :], wgu[:, pl.ds(pl.multiple_of(a * 512, 512), 512)], 1, 0)
            d = dot(rowcot[chunk_rows, :], wd[pl.ds(pl.multiple_of(a * 256, 256), 256), :], 1, 1)
            for i in range(n):
                for h in range(2):
                    gu_h = gu[i * ROWS : (i + 1) * ROWS, 256 * h : 256 * h + 256]
                    d_h = d[i * ROWS : (i + 1) * ROWS, HID * h : HID * h + HID]
                    if j == 0:
                        own[at, i, h, :, pl.ds(0, 256)] = gu_h
                        own[at, i, h, :, pl.ds(256, HID)] = d_h
                    else:
                        part[at, i, j - 1, h, :, pl.ds(0, 256)] = gu_h.astype(BF)
                        part[at, i, j - 1, h, :, pl.ds(256, HID)] = d_h.astype(BF)
            if j == 2:
                rs1(t, n, 0).start()
                rs1(t, n, 1).start()

    def pass_sums(t, n):
        at = lax.rem(t, 3)
        first = first_of(t)
        for h in range(2):
            rs1(t, n, h).wait_recv()
            for i in range(n):
                part[at, i, 2 * h, h] = (part[at, i, 2 * h, h].astype(F32) + r1[first + i, h].astype(F32)).astype(BF)
            rs2(t, n, h).start()

    def pointwise(t, n):
        at = lax.rem(t, 3)
        first = first_of(t)
        rs2(t, n, 0).wait_recv()
        rs2(t, n, 1).wait_recv()
        for i in range(n):
            scale = scl[first + i]
            for h in range(2):
                v = own[at, i, h] + r2[first + i, 0, h].astype(F32) + r2[first + i, 1, h].astype(F32)
                gate, up, down = v[:, :HID], v[:, HID : 2 * HID], v[:, 2 * HID :]
                sig = jax.nn.sigmoid(gate)
                act = gate * sig
                slope = sig * (1.0 + gate * (1.0 - sig))
                dh = down * scale
                g = 2 * x + h
                ag[first + i, g, :, pl.ds(0, HID)] = (dh * up * slope).astype(BF)
                ag[first + i, g, :, pl.ds(HID, HID)] = (dh * act).astype(BF)
                ag[first + i, g, :, pl.ds(2 * HID, HID)] = (act * up * scale).astype(BF)
        ag1(t, n, 0).start()
        ag1(t, n, 1).start()

    def pass_shares(t, n):
        for side in range(2):
            ag1_wait(t, n, side)
            ag2(t, n, side).start()

    def backward(t, n):
        ag2_wait(t, n, 0)
        ag2_wait(t, n, 1)
        first = first_of(t)
        grads = []
        for i in range(n):
            rows = pl.ds(pl.multiple_of((first + i) * ROWS, 16), ROWS)
            for g in range(8):
                hs[rows, pl.ds(g * HID, HID)] = ag[first + i, g, :, pl.ds(2 * HID, HID)]
            grads.append(jnp.concatenate([ag[first + i, g, :, pl.ds(0, 2 * HID)] for g in range(8)], axis=1))
        grads = jnp.concatenate(grads, axis=0) if n > 1 else grads[0]
        rowact[pl.ds(0, n * ROWS), :] = dot(grads, wgu[...], 1, 1).astype(BF)

        core0 = lax.broadcasted_iota(jnp.int32, (ROWS, width), 0) < CAP
        for k, elements in enumerate(CHUNK):
            if len(elements) != n:
                continue

            @pl.when(t == k)
            def _():
                for i, (da, db) in enumerate(elements):
                    k0, k1 = ORDER.index((da, db)), ORDER.index((db, da))
                    out = rowact[pl.ds(i * ROWS, ROWS), :]
                    if k0 < k1:
                        rets[k0] = out
                        rets[k1] = out
                    elif k0 == k1:
                        rets[k0] = out
                        ret_copy(k0).start()
                    else:
                        wide = out.astype(F32)
                        rets[k0] = jnp.where(core0, wide, rets[k0].astype(F32)).astype(BF)
                        rets[k1] = jnp.where(core0, rets[k1].astype(F32), wide).astype(BF)
                        ret_copy(k0).start()
                        ret_copy(k1).start()

    def on(cond, f, *args):
        @pl.when(cond)
        def _():
            f(*args)

    def any_size(t, f):
        on((t >= 1) & (t < LAST), f, t, 2)
        on(t == LAST, f, t, 1)

    def after(s, op):
        for k, name in PASS_ON:
            if name != op or (k == 0) != isinstance(s, int):
                continue
            if k == 0:
                act_on(PASS_ON[k, name])
            else:
                on(s == k, act_on, PASS_ON[k, name])

    load_stage(CHUNK[0])
    own_ext = gext.at[1 - c, 0]
    pltpu.make_async_copy(own_ext, own_ext, xrecv.at[0]).wait()
    ext_now[0] = gext[:, 0, :, pl.ds(0, TOK)]
    after(0, "L")
    for cp in wcopies:
        cp.wait()
    forward(0, 1)
    after(0, "F")
    for n in range(1, CHIPS):
        ref = gext.at[c, n]
        pltpu.make_async_copy(ref, ref, xrecv.at[n]).wait()
    ext_relay().start()
    pass_sums(0, 1)
    after(0, "S")
    pointwise(0, 1)
    after(0, "P")
    for core in range(2):
        ext = ext_now[0, core].astype(F32)
        for k, (dz, dy) in enumerate(ORDER):
            expert = (2 * chip_at(-dz % SIDE, -dy % SIDE) + c).astype(F32)
            pick, _ = routing(ext, expert, core)
            sall[pl.ds(k * ROWS, ROWS), pl.ds(core * TOK, TOK)] = pick.astype(BF)
    after(0, "sall")
    ext_relay().wait_recv()

    def step(s, carry):
        any_size(s - 2, pointwise)
        after(s, "P")
        any_size(s - 1, pass_sums)
        after(s, "S")
        on((s >= 4) & (s < LAST + 3), backward, s - 3, 2)
        on((s == 3) | (s == LAST + 3), backward, s - 3, 1)
        after(s, "B")
        for k in range(1, LAST + 1):
            on(s == k, load_stage, CHUNK[k])
        after(s, "L")
        on(s == 3, sends_done, 0, 1)
        on((s >= 4) & (s <= LAST), sends_done, s - 3, 2)
        any_size(s, forward)
        after(s, "F")
        on(s == 2, pass_shares, 0, 1)
        any_size(s - 2, pass_shares)
        after(s, "H")
        return carry

    lax.fori_loop(1, LAST + 4, step, 0)

    live_total = jnp.zeros((2 * TOP, TOK), F32)
    for core in range(2):
        for n in range(CHIPS):
            live_total += gext[core, n, :, pl.ds(TOK, TOK)].astype(F32)
    factor = float(2 * CHIPS * TOK) / live_total[0:1, 0:1]
    outs = []
    for f in range(4):
        if f >= 2:
            outs[f - 2].wait()
        dgt[f % 2] = (dot(hs[:, pl.ds(256 * f, 256)], rowcot[...], 0, 0) * factor).astype(BF)
        cp = pltpu.make_async_copy(dgt.at[f % 2], down_grad.at[0, pl.ds(256 * f, 256), :], osem.at[f % 2])
        cp.start()
        outs.append(cp)

    for k in range(CHIPS):
        pltpu.make_async_copy(retr.at[k], retr.at[k], rtr.at[k]).wait()
    dense[...] = dot(sall[...], retr[...].reshape(CHIPS * ROWS, width), 0, 0)
    swap = pltpu.make_async_remote_copy(
        src_ref=dense.at[pl.ds(pl.multiple_of((1 - c) * TOK, TOK), TOK)],
        dst_ref=sibr,
        send_sem=css.at[0],
        recv_sem=csr.at[0],
        device_id=sibling,
        device_id_type=MESH,
    )
    swap.start()
    swap.wait()
    kept = dense[pl.ds(pl.multiple_of(c * TOK, TOK), TOK), :]
    igt[...] = ((kept + sibr[...]) * factor).astype(BF)
    final = pltpu.make_async_copy(igt, in_grad, osem.at[2])
    final.start()

    final.wait()
    outs[2].wait()
    outs[3].wait()
    for n, what in enumerate(sends):
        half_copy(n, *what).wait_send()
    for n, what in enumerate(sib_copies):
        sibling_copy(n, *what).wait_send()
    for k in range(1, CHIPS):
        ret_copy(k).wait_send()

    for at in offsets:
        ext_copy(*at).wait_send()
    ext_relay().wait_send()
    for t in (6, 7):
        sends_done(t, 2)
    sends_done(LAST, 1)

    def drain(t, n):
        for h in range(2):
            ag1(t, n, h).wait_send()
            ag2(t, n, h).wait_send()

    def drain_pair(t, carry):
        drain(t, 2)
        return carry

    drain(0, 1)
    lax.fori_loop(1, LAST, drain_pair, 0)
    drain(LAST, 1)


def local(
    activations, cotangent, expert_ids, combine, log_ratio, valid_mask, segment_ids, w_gate, w_up, w_down
):
    tok_rows, width = activations.shape
    any_spec = pl.BlockSpec(memory_space=pl.ANY)
    dma = pltpu.SemaphoreType.DMA
    in_grad, down_grad, _ = pl.pallas_call(
        kernel,
        out_shape=(
            jax.ShapeDtypeStruct((tok_rows, width), BF),
            jax.ShapeDtypeStruct(w_down.shape, BF),
            jax.ShapeDtypeStruct((2, CHIPS, BLOCK, width), BF),
        ),
        in_specs=[any_spec] * 2 + [pl.BlockSpec(memory_space=pltpu.VMEM)] * 5 + [any_spec] * 3,
        out_specs=(any_spec,) * 3,
        scratch_shapes=[
            pltpu.VMEM((width, 2048), BF),
            pltpu.VMEM((1024, width), BF),
            pltpu.VMEM((BLOCK, width), BF),
            pltpu.VMEM((2, CHIPS, 2 * TOP, 2 * TOK), BF),
            pltpu.VMEM((2, 2, 2 * TOP, TOK), BF),
            pltpu.VMEM((2, 2, BLOCK, width), BF),
            pltpu.VMEM((2 * ROWS, width), BF),
            pltpu.VMEM((CHIPS * ROWS, width), BF),
            pltpu.VMEM((CHIPS, ROWS, HID), F32),
            pltpu.VMEM((3, 2, 3, 2, ROWS, LANES), BF),
            pltpu.VMEM((3, 2, 2, ROWS, LANES), F32),
            pltpu.VMEM((CHIPS, 2, ROWS, LANES), BF),
            pltpu.VMEM((CHIPS, 2, 2, ROWS, LANES), BF),
            pltpu.VMEM((CHIPS, 8, ROWS, LANES), BF),
            pltpu.VMEM((CHIPS * ROWS, 1024), BF),
            pltpu.VMEM((CHIPS, ROWS, width), BF),
            pltpu.VMEM((CHIPS, ROWS, width), BF),
            pltpu.VMEM((2 * TOK, width), F32),
            pltpu.VMEM((TOK, width), F32),
            pltpu.VMEM((CHIPS * ROWS, 2 * TOK), BF),
            pltpu.VMEM((2, 256, width), BF),
            pltpu.VMEM((TOK, width), BF),
            dma((17,)), dma((4,)), dma((CHIPS + 1,)), dma((CHIPS + 1,)),
            dma((26 * 2,)), dma((CHIPS, 2)), dma((CHIPS,)), dma((CHIPS,)),
            dma((LAST + 1, 2)), dma((LAST + 1, 2)), dma((LAST + 1, 2)), dma((LAST + 1, 2)),
            dma((LAST + 1, 2)), dma((LAST + 1, 2)), dma((LAST + 1, 2)), dma((LAST + 1, 2)),
            dma((CHIPS,)), dma((CHIPS,)), dma((1,)), dma((1,)), dma((3,)),
        ],
        compiler_params=pltpu.CompilerParams(
            collective_id=0, has_side_effects=True, vmem_limit_bytes=63 * 2**20
        ),
        cost_estimate=pl.CostEstimate(flops=28_200_000_000, bytes_accessed=60_000_000, transcendentals=1_000_000),
    )(
        activations, cotangent, expert_ids.T, combine.T, log_ratio[None], valid_mask[None], segment_ids[None],
        w_gate, w_up, w_down,
    )
    return in_grad, down_grad


def solution(mesh):
    return jax.shard_map(
        local,
        mesh=mesh,
        in_specs=(
            P("expert", "tensor"),
            P("expert", "tensor"),
            P("expert", None),
            P("expert", None),
            P("expert"),
            P("expert"),
            P("expert"),
            P("expert", "tensor", None),
            P("expert", "tensor", None),
            P("expert", None, "tensor"),
        ),
        out_specs=(P("expert", "tensor"), P("expert", None, "tensor")),
        check_vma=False,
    )
```

```python
import functools

import jax
import jax.numpy as jnp
from jax import lax
from jax.experimental import pallas as pl
from jax.experimental.pallas import tpu as pltpu
from jax.sharding import PartitionSpec as P

BF = jnp.bfloat16
F32 = jnp.float32
MESH = pl.DeviceIdType.MESH

SIDE = 4
CHIPS = SIDE * SIDE
CAP = 40
TOK = 128
ROWS = 2 * CAP
TOP = 8
HID = 128
LANES = 3 * HID
BLOCK = 2 * TOK
LAST = 8

ORDER = [
    (0, 0),
    (1, 0), (3, 0),
    (0, 1), (0, 3),
    (1, 3), (1, 1),
    (3, 3), (3, 1),
    (2, 1), (1, 2),
    (3, 2), (2, 3),
    (2, 0), (0, 2),
    (2, 2),
]
CHUNK = [ORDER[:1]] + [ORDER[i : i + 2] for i in range(1, 15, 2)] + [ORDER[15:]]
PASS_ON = {
    (0, "S"): [
        ("full", (0, 0), 1),
    ],
    (0, "P"): [
        ("wait", (3, 0)),
        ("wait", (1, 0)),
    ],
    (1, "L"): [
        ("full", (1, 0), 1),
    ],
    (1, "F"): [
        ("wait", (0, 1)),
        ("half", (3, 0), 0, 1, 0),
        ("wait", (0, 3)),
    ],
    (2, "L"): [
        ("full", (3, 0), 1),
    ],
    (3, "P"): [
        ("wait", (1, 1)),
        ("wait", (1, 3)),
        ("half", (1, 0), 0, -1, 1),
    ],
    (3, "B"): [
        ("half", (1, 1), 1, -1, 1),
    ],
    (3, "L"): [
        ("half", (1, 3), 1, 1, 0),
    ],
    (3, "F"): [
        ("wait", (3, 3)),
    ],
    (4, "P"): [
        ("half", (0, 1), 1, -1, 1),
        ("wait", (3, 1)),
        ("wait", (2, 0)),
    ],
    (4, "S"): [
        ("half", (0, 3), 1, 1, 0),
        ("full", (2, 0), 1),
    ],
    (4, "L"): [
        ("half", (3, 1), 1, -1, 1),
    ],
    (4, "F"): [
        ("wait", (1, 2)),
    ],
    (4, "H"): [
        ("half", (3, 3), 1, 1, 0),
    ],
    (5, "P"): [
        ("wait", (2, 1)),
    ],
    (5, "B"): [
        ("wait", (3, 2)),
    ],
    (5, "L"): [
        ("half", (2, 1), 1, -1, 1),
    ],
    (5, "F"): [
        ("wait", (2, 3)),
    ],
    (6, "F"): [
        ("half", (2, 3), 1, 1, 0),
    ],
    (7, "P"): [
        ("wait", (2, 2)),
        ("wait", (0, 2)),
    ],
}
HALVES = (pl.ds(0, TOK), pl.ds(TOK, BLOCK - TOK))


def first_of(t):
    return max(2 * t - 1, 0) if isinstance(t, int) else 2 * t - lax.div(t + 8, 9)


def dot(a, b, ca, cb):
    return lax.dot_general(a, b, (((ca,), (cb,)), ((), ())), preferred_element_type=F32)


def kernel(
    acts, cots, ids, combine, log_ratio, valid, segments, w_gate, w_up, w_down,
    in_grad, down_grad, gbuf,
    wgu, wd, mine, gext, ext_now, stage, rowact, rowcot, scl, part, own, r1, r2, ag, hs, rets, retr, dense, sibr, late, slate, sall,
    dgt, igt,
    wsem, stsem, xsend, xrecv, gsend, grecv, bsend, brecv, r1s, r1r, r2s, r2r, a1s, a1r, a2s, a2r, rts, rtr,
    css, csr, osem,
):
    e = lax.axis_index("expert")
    x = lax.axis_index("tensor")
    c = lax.rem(e, 2)
    chip = lax.div(e, 2)
    z = lax.div(chip, SIDE)
    y = lax.rem(chip, SIDE)
    width = acts.shape[1]
    right = lax.rem(x + 1, SIDE)
    left = lax.rem(x + SIDE - 1, SIDE)

    def chip_at(dz, dy):
        return lax.rem(z + dz, SIDE) * SIDE + lax.rem(y + dy, SIDE)

    def peer(dz, dy):
        return (chip_at(dz, dy) * 2 + c, x)

    sibling = (chip * 2 + 1 - c, x)

    def zy(da, db):
        return da * (1 - c) + db * c, da * c + db * (1 - c)

    def slot(da, db):
        dz, dy = zy(da % SIDE, db % SIDE)
        return dz * SIDE + dy

    bar = pltpu.get_barrier_semaphore()
    partners = [(e, right), (e, left), sibling]
    partners += [peer(dz, dy) for dz in range(SIDE) for dy in range(SIDE) if (dz, dy) != (0, 0)]
    for p in partners:
        pl.semaphore_signal(bar, inc=1, device_id=p, device_id_type=MESH)

    wcopies = []
    for g in range(8):
        cols = pl.ds(g * HID, HID)
        wcopies.append(
            pltpu.make_async_copy(w_gate.at[0, :, cols], wgu.at[:, pl.ds(2 * g * HID, HID)], wsem.at[2 * g])
        )
        wcopies.append(
            pltpu.make_async_copy(w_up.at[0, :, cols], wgu.at[:, pl.ds((2 * g + 1) * HID, HID)], wsem.at[2 * g + 1])
        )
    wcopies.append(pltpu.make_async_copy(w_down.at[0], wd, wsem.at[16]))
    loads = [
        pltpu.make_async_copy(acts, mine.at[pl.ds(0, TOK)], stsem.at[0]),
        pltpu.make_async_copy(cots, mine.at[pl.ds(TOK, TOK)], stsem.at[1]),
    ]
    for cp in loads + wcopies:
        cp.start()

    lane = lax.broadcasted_iota(jnp.int32, (TOP, TOK), 1)
    seg = jnp.broadcast_to(segments[...], (TOP, TOK))
    following = pltpu.roll(seg, TOK - 1, 1)
    final_dev = (e + 1) // (2 * CHIPS)
    closing = jnp.where(lane == TOK - 1, final_dev, (following != seg).astype(jnp.int32))
    live = jnp.maximum(jnp.broadcast_to(valid[...], (TOP, TOK)), closing).astype(F32)
    weight = jnp.minimum(jnp.exp(jnp.broadcast_to(log_ratio[...], (TOP, TOK))), 2.0) * live
    slot_scale = (combine[...] * weight).astype(BF)
    count = jnp.broadcast_to(jnp.sum(live, axis=1, keepdims=True), (TOP, TOK)).astype(BF)
    ids_scales = jnp.concatenate([ids[...].astype(F32).astype(BF), slot_scale], axis=0)
    gext[c, 0, :, pl.ds(0, TOK)] = ids_scales
    gext[c, 0, :, pl.ds(TOK, TOK)] = jnp.concatenate([count, count], axis=0)
    for cp in loads:
        cp.wait()
    pl.semaphore_wait(bar, len(partners))

    sends = []

    def block_at(da, db):
        if (da % SIDE, db % SIDE) == (0, 0):
            return mine
        return gbuf.at[c, slot(da, db)]

    def half_copy(n, da, db, axis, by, half):
        na, nb = (da - by, db) if axis == 0 else (da, db - by)
        ta, tb = (by, 0) if axis == 0 else (0, by)
        dz, dy = zy(ta % SIDE, tb % SIDE)
        return pltpu.make_async_remote_copy(
            src_ref=block_at(da, db).at[HALVES[half]],
            dst_ref=gbuf.at[c, slot(na, nb), HALVES[half]],
            send_sem=gsend.at[n],
            recv_sem=grecv.at[slot(na, nb), half],
            device_id=peer(dz, dy),
            device_id_type=MESH,
        )

    def send_half(*what):
        half_copy(len(sends), *what).start()
        sends.append(what)

    def send_full(da, db, axis):
        for by in (1, -1):
            for half in (0, 1):
                send_half(da, db, axis, by, half)

    sib_copies = []

    def sibling_copy(n, da, db):
        return pltpu.make_async_remote_copy(
            src_ref=block_at(da, db),
            dst_ref=gbuf.at[c, slot(da, db)],
            send_sem=bsend.at[n],
            recv_sem=brecv.at[slot(da, db)],
            device_id=sibling,
            device_id_type=MESH,
        )

    def send_sibling(*what):
        sibling_copy(len(sib_copies), *what).start()
        sib_copies.append(what)

    def wait_half(da, db, half):
        ref = gbuf.at[c, slot(da, db), HALVES[half]]
        pltpu.make_async_copy(ref, ref, grecv.at[slot(da, db), half]).wait()

    def act_on(events):
        for kind, at, *rest in events:
            if kind == "wait":
                wait_half(*at, 0)
                wait_half(*at, 1)
                send_sibling(*at)
            elif kind == "full":
                send_full(*at, *rest)
            else:
                send_half(*at, *rest)

    def ext_copy(dz, dy):
        n = dz * SIDE + dy
        to = (-dz % SIDE) * SIDE + -dy % SIDE
        return pltpu.make_async_remote_copy(
            src_ref=gext.at[c, 0], dst_ref=gext.at[c, to], send_sem=xsend.at[n], recv_sem=xrecv.at[to],
            device_id=sibling if n == 0 else peer(dz, dy), device_id_type=MESH,
        )

    def ext_relay():
        others = gext.at[c, pl.ds(1, CHIPS - 1)]
        return pltpu.make_async_remote_copy(
            src_ref=others, dst_ref=others, send_sem=xsend.at[CHIPS], recv_sem=xrecv.at[CHIPS],
            device_id=sibling, device_id_type=MESH,
        )

    offsets = [(dz, dy) for dz in range(SIDE) for dy in range(SIDE)]
    ext_copy(0, 0).start()
    send_sibling(0, 0)
    for at in offsets[1:]:
        ext_copy(*at).start()
    send_full(0, 0, 0)

    row_i = lax.broadcasted_iota(jnp.int32, (TOK, TOK), 0)
    col_i = lax.broadcasted_iota(jnp.int32, (TOK, TOK), 1)
    upper = (row_i < col_i).astype(BF)
    slot_iota = lax.broadcasted_iota(jnp.int32, (ROWS, TOK), 0).astype(F32)

    def routing(ext, expert, core):
        hit = (ext[0:TOP] == expert).astype(F32)
        mask = jnp.sum(hit, axis=0, keepdims=True)
        scale = jnp.sum(hit * ext[TOP : 2 * TOP], axis=0, keepdims=True)
        rank = dot(jnp.broadcast_to(mask, (16, TOK)).astype(BF), upper, 1, 0)[0:1]
        key = jnp.where(mask > 0.5, rank + float(CAP * core), -1.0)
        return (slot_iota == key).astype(F32), scale

    def remote_x(src, dst, ssem, rsem, to):
        return pltpu.make_async_remote_copy(
            src_ref=src, dst_ref=dst, send_sem=ssem, recv_sem=rsem, device_id=(e, to), device_id_type=MESH
        )

    def rs1(t, n, h):
        return remote_x(
            part.at[lax.rem(t, 3), pl.ds(0, n), 1, h], r1.at[pl.ds(first_of(t), n), h],
            r1s.at[t, h], r1r.at[t, h], (right, left)[h],
        )

    def rs2(t, n, side):
        return remote_x(
            part.at[lax.rem(t, 3), pl.ds(0, n), 2 * side], r2.at[pl.ds(first_of(t), n), side],
            r2s.at[t, side], r2r.at[t, side], (right, left)[side],
        )

    def ag1(t, n, side):
        ref = ag.at[pl.ds(first_of(t), n), pl.ds(2 * x, 2)]
        return remote_x(ref, ref, a1s.at[t, side], a1r.at[t, side], (right, left)[side])

    def ag1_wait(t, n, side):
        ref = ag.at[pl.ds(first_of(t), n), pl.ds(2 * (left, right)[side], 2)]
        pltpu.make_async_copy(ref, ref, a1r.at[t, side]).wait()

    def ag2(t, n, side):
        ref = ag.at[pl.ds(first_of(t), n), 2 * (left, right)[side] + side]
        return remote_x(ref, ref, a2s.at[t, side], a2r.at[t, side], (right, left)[side])

    def ag2_wait(t, n, side):
        ref = ag.at[pl.ds(first_of(t), n), 2 * lax.rem(x + 2, SIDE) + side]
        pltpu.make_async_copy(ref, ref, a2r.at[t, side]).wait()

    def ret_copy(k):
        dz, dy = ORDER[k]
        if k == 0:
            return pltpu.make_async_copy(rets.at[0], retr.at[0], rtr.at[0])
        return pltpu.make_async_remote_copy(
            src_ref=rets.at[k], dst_ref=retr.at[k], send_sem=rts.at[k], recv_sem=rtr.at[k],
            device_id=peer(dz, dy), device_id_type=MESH,
        )

    def load_stage(elements):
        copies = []
        for i, at in enumerate(elements):
            da, db = at
            if at != (0, 0):
                ext_now[i, 0] = gext[0, da * SIDE + db, :, pl.ds(0, TOK)]
                ext_now[i, 1] = gext[1, db * SIDE + da, :, pl.ds(0, TOK)]
            theirs = (da * c + db * (1 - c)) * SIDE + da * (1 - c) + db * c
            ref = gbuf.at[1 - c, theirs]
            pltpu.make_async_copy(ref, ref, brecv.at[theirs]).wait()
            copies.append(pltpu.make_async_copy(block_at(*at), stage.at[i, c], stsem.at[2 * i]))
            copies.append(pltpu.make_async_copy(ref, stage.at[i, 1 - c], stsem.at[2 * i + 1]))
        for cp in copies:
            cp.start()
        for cp in copies:
            cp.wait()

    def sends_done(t, n):
        for h in range(2):
            rs1(t, n, h).wait_send()
            rs2(t, n, h).wait_send()

    def forward(t, n):
        first = first_of(t)
        expert = e.astype(F32)
        for i in range(n):
            picks, scales = [], []
            for core in range(2):
                pick, scale = routing(ext_now[i, core].astype(F32), expert, core)
                picks.append(pick)
                scales.append(jnp.sum(pick * scale, axis=1, keepdims=True))
            pick = jnp.concatenate(picks, axis=1).astype(BF)
            rows = pl.ds(pl.multiple_of((first + i) * ROWS, 16), ROWS)
            scl[first + i] = jnp.broadcast_to(scales[0] + scales[1], (ROWS, HID))
            act = jnp.concatenate([stage[i, 0, pl.ds(0, TOK), :], stage[i, 1, pl.ds(0, TOK), :]], axis=0)
            rowact[pl.ds(i * ROWS, ROWS), :] = dot(pick, act, 1, 0).astype(BF)
            cot = jnp.concatenate([stage[i, 0, pl.ds(TOK, TOK), :], stage[i, 1, pl.ds(TOK, TOK), :]], axis=0)
            rowcot[rows, :] = dot(pick, cot, 1, 0).astype(BF)

        at = lax.rem(t, 3)
        chunk_rows = pl.ds(pl.multiple_of(first * ROWS, 16), n * ROWS)
        for j in (2, 1, 3, 0):
            a = lax.rem(x + j, SIDE)
            gu = dot(rowact[pl.ds(0, n * ROWS), :], wgu[:, pl.ds(pl.multiple_of(a * 512, 512), 512)], 1, 0)
            d = dot(rowcot[chunk_rows, :], wd[pl.ds(pl.multiple_of(a * 256, 256), 256), :], 1, 1)
            for i in range(n):
                for h in range(2):
                    gu_h = gu[i * ROWS : (i + 1) * ROWS, 256 * h : 256 * h + 256]
                    d_h = d[i * ROWS : (i + 1) * ROWS, HID * h : HID * h + HID]
                    if j == 0:
                        own[at, i, h, :, pl.ds(0, 256)] = gu_h
                        own[at, i, h, :, pl.ds(256, HID)] = d_h
                    else:
                        part[at, i, j - 1, h, :, pl.ds(0, 256)] = gu_h.astype(BF)
                        part[at, i, j - 1, h, :, pl.ds(256, HID)] = d_h.astype(BF)
            if j == 2:
                rs1(t, n, 0).start()
                rs1(t, n, 1).start()

    def pass_sums(t, n):
        at = lax.rem(t, 3)
        first = first_of(t)
        for h in range(2):
            rs1(t, n, h).wait_recv()
            for i in range(n):
                part[at, i, 2 * h, h] = (part[at, i, 2 * h, h].astype(F32) + r1[first + i, h].astype(F32)).astype(BF)
            rs2(t, n, h).start()

    def pointwise(t, n):
        at = lax.rem(t, 3)
        first = first_of(t)
        rs2(t, n, 0).wait_recv()
        rs2(t, n, 1).wait_recv()
        for i in range(n):
            scale = scl[first + i]
            for h in range(2):
                v = own[at, i, h] + r2[first + i, 0, h].astype(F32) + r2[first + i, 1, h].astype(F32)
                gate, up, down = v[:, :HID], v[:, HID : 2 * HID], v[:, 2 * HID :]
                sig = jax.nn.sigmoid(gate)
                act = gate * sig
                slope = sig * (1.0 + gate * (1.0 - sig))
                dh = down * scale
                g = 2 * x + h
                ag[first + i, g, :, pl.ds(0, HID)] = (dh * up * slope).astype(BF)
                ag[first + i, g, :, pl.ds(HID, HID)] = (dh * act).astype(BF)
                ag[first + i, g, :, pl.ds(2 * HID, HID)] = (act * up * scale).astype(BF)
        ag1(t, n, 0).start()
        ag1(t, n, 1).start()

    def pass_shares(t, n):
        for side in range(2):
            ag1_wait(t, n, side)
            ag2(t, n, side).start()

    def backward(t, n):
        ag2_wait(t, n, 0)
        ag2_wait(t, n, 1)
        first = first_of(t)
        grads = []
        for i in range(n):
            rows = pl.ds(pl.multiple_of((first + i) * ROWS, 16), ROWS)
            for g in range(8):
                hs[rows, pl.ds(g * HID, HID)] = ag[first + i, g, :, pl.ds(2 * HID, HID)]
            grads.append(jnp.concatenate([ag[first + i, g, :, pl.ds(0, 2 * HID)] for g in range(8)], axis=1))
        grads = jnp.concatenate(grads, axis=0) if n > 1 else grads[0]
        rowact[pl.ds(0, n * ROWS), :] = dot(grads, wgu[...], 1, 1).astype(BF)

        core0 = lax.broadcasted_iota(jnp.int32, (ROWS, width), 0) < CAP
        for k, elements in enumerate(CHUNK):
            if len(elements) != n:
                continue

            @pl.when(t == k)
            def _():
                for i, (da, db) in enumerate(elements):
                    k0, k1 = ORDER.index((da, db)), ORDER.index((db, da))
                    out = rowact[pl.ds(i * ROWS, ROWS), :]
                    if k0 < k1:
                        rets[k0] = out
                        rets[k1] = out
                    elif k0 == k1:
                        rets[k0] = out
                        ret_copy(k0).start()
                    else:
                        wide = out.astype(F32)
                        rets[k0] = jnp.where(core0, wide, rets[k0].astype(F32)).astype(BF)
                        rets[k1] = jnp.where(core0, rets[k1].astype(F32), wide).astype(BF)
                        ret_copy(k0).start()
                        ret_copy(k1).start()

    def on(cond, f, *args):
        @pl.when(cond)
        def _():
            f(*args)

    def any_size(t, f):
        on((t >= 1) & (t < LAST), f, t, 2)
        on(t == LAST, f, t, 1)

    def after(s, op):
        for k, name in PASS_ON:
            if name != op or (k == 0) != isinstance(s, int):
                continue
            if k == 0:
                act_on(PASS_ON[k, name])
            else:
                on(s == k, act_on, PASS_ON[k, name])

    load_stage(CHUNK[0])
    own_ext = gext.at[1 - c, 0]
    pltpu.make_async_copy(own_ext, own_ext, xrecv.at[0]).wait()
    ext_now[0] = gext[:, 0, :, pl.ds(0, TOK)]
    after(0, "L")
    for cp in wcopies:
        cp.wait()
    forward(0, 1)
    after(0, "F")
    for n in range(1, CHIPS):
        ref = gext.at[c, n]
        pltpu.make_async_copy(ref, ref, xrecv.at[n]).wait()
    ext_relay().start()
    pass_sums(0, 1)
    after(0, "S")
    pointwise(0, 1)
    after(0, "P")
    for core in range(2):
        ext = ext_now[0, core].astype(F32)
        for k, (dz, dy) in enumerate(ORDER):
            expert = (2 * chip_at(-dz % SIDE, -dy % SIDE) + c).astype(F32)
            pick, _ = routing(ext, expert, core)
            sall[pl.ds(k * ROWS, ROWS), pl.ds(core * TOK, TOK)] = pick.astype(BF)
    dz, dy = ORDER[-1]
    twin = (2 * chip_at(-dz % SIDE, -dy % SIDE) + 1 - c).astype(F32)
    pick0, _ = routing(ext_now[0, 0].astype(F32), twin, 0)
    pick1, _ = routing(ext_now[0, 1].astype(F32), twin, 1)
    slate[...] = jnp.where(c == 0, pick0, pick1).astype(BF)
    after(0, "sall")
    ext_relay().wait_recv()

    def step(s, carry):
        any_size(s - 2, pointwise)
        after(s, "P")
        any_size(s - 1, pass_sums)
        after(s, "S")
        on((s >= 4) & (s < LAST + 3), backward, s - 3, 2)
        on((s == 3) | (s == LAST + 3), backward, s - 3, 1)
        after(s, "B")
        for k in range(1, LAST + 1):
            on(s == k, load_stage, CHUNK[k])
        after(s, "L")
        on(s == 3, sends_done, 0, 1)
        on((s >= 4) & (s <= LAST), sends_done, s - 3, 2)
        any_size(s, forward)
        after(s, "F")
        on(s == 2, pass_shares, 0, 1)
        any_size(s - 2, pass_shares)
        after(s, "H")
        return carry

    lax.fori_loop(1, LAST + 4, step, 0)

    live_total = jnp.zeros((2 * TOP, TOK), F32)
    for core in range(2):
        for n in range(CHIPS):
            live_total += gext[core, n, :, pl.ds(TOK, TOK)].astype(F32)
    factor = float(2 * CHIPS * TOK) / live_total[0:1, 0:1]
    outs = []
    for f in range(4):
        if f >= 2:
            outs[f - 2].wait()
        dgt[f % 2] = (dot(hs[:, pl.ds(256 * f, 256)], rowcot[...], 0, 0) * factor).astype(BF)
        cp = pltpu.make_async_copy(dgt.at[f % 2], down_grad.at[0, pl.ds(256 * f, 256), :], osem.at[f % 2])
        cp.start()
        outs.append(cp)

    def returned(k):
        pltpu.make_async_copy(retr.at[k], retr.at[k], rtr.at[k]).wait()

    for k in range(CHIPS - 1):
        returned(k)
    early = (CHIPS - 1) * ROWS
    dense[...] = dot(sall[pl.ds(0, early), :], retr[pl.ds(0, CHIPS - 1)].reshape(early, width), 0, 0)
    swap = pltpu.make_async_remote_copy(
        src_ref=dense.at[pl.ds(pl.multiple_of((1 - c) * TOK, TOK), TOK)],
        dst_ref=sibr,
        send_sem=css.at[0],
        recv_sem=csr.at[0],
        device_id=sibling,
        device_id_type=MESH,
    )
    swap.start()
    returned(CHIPS - 1)
    relay = pltpu.make_async_remote_copy(
        src_ref=retr.at[CHIPS - 1],
        dst_ref=late,
        send_sem=css.at[1],
        recv_sem=csr.at[1],
        device_id=sibling,
        device_id_type=MESH,
    )
    relay.start()
    own_lanes = pl.ds(pl.multiple_of(c * TOK, TOK), TOK)
    total = dense[own_lanes, :] + dot(sall[pl.ds(early, ROWS), own_lanes], retr[CHIPS - 1], 0, 0)
    swap.wait()
    relay.wait()
    total = total + sibr[...] + dot(slate[...], late[...], 0, 0)
    igt[...] = (total * factor).astype(BF)
    final = pltpu.make_async_copy(igt, in_grad, osem.at[2])
    final.start()

    final.wait()
    outs[2].wait()
    outs[3].wait()
    for n, what in enumerate(sends):
        half_copy(n, *what).wait_send()
    for n, what in enumerate(sib_copies):
        sibling_copy(n, *what).wait_send()
    for k in range(1, CHIPS):
        ret_copy(k).wait_send()

    for at in offsets:
        ext_copy(*at).wait_send()
    ext_relay().wait_send()
    for t in (6, 7):
        sends_done(t, 2)
    sends_done(LAST, 1)

    def drain(t, n):
        for h in range(2):
            ag1(t, n, h).wait_send()
            ag2(t, n, h).wait_send()

    def drain_pair(t, carry):
        drain(t, 2)
        return carry

    drain(0, 1)
    lax.fori_loop(1, LAST, drain_pair, 0)
    drain(LAST, 1)


def local(
    activations, cotangent, expert_ids, combine, log_ratio, valid_mask, segment_ids, w_gate, w_up, w_down
):
    tok_rows, width = activations.shape
    any_spec = pl.BlockSpec(memory_space=pl.ANY)
    dma = pltpu.SemaphoreType.DMA
    in_grad, down_grad, _ = pl.pallas_call(
        kernel,
        out_shape=(
            jax.ShapeDtypeStruct((tok_rows, width), BF),
            jax.ShapeDtypeStruct(w_down.shape, BF),
            jax.ShapeDtypeStruct((2, CHIPS, BLOCK, width), BF),
        ),
        in_specs=[any_spec] * 2 + [pl.BlockSpec(memory_space=pltpu.VMEM)] * 5 + [any_spec] * 3,
        out_specs=(any_spec,) * 3,
        scratch_shapes=[
            pltpu.VMEM((width, 2048), BF),
            pltpu.VMEM((1024, width), BF),
            pltpu.VMEM((BLOCK, width), BF),
            pltpu.VMEM((2, CHIPS, 2 * TOP, 2 * TOK), BF),
            pltpu.VMEM((2, 2, 2 * TOP, TOK), BF),
            pltpu.VMEM((2, 2, BLOCK, width), BF),
            pltpu.VMEM((2 * ROWS, width), BF),
            pltpu.VMEM((CHIPS * ROWS, width), BF),
            pltpu.VMEM((CHIPS, ROWS, HID), F32),
            pltpu.VMEM((3, 2, 3, 2, ROWS, LANES), BF),
            pltpu.VMEM((3, 2, 2, ROWS, LANES), F32),
            pltpu.VMEM((CHIPS, 2, ROWS, LANES), BF),
            pltpu.VMEM((CHIPS, 2, 2, ROWS, LANES), BF),
            pltpu.VMEM((CHIPS, 8, ROWS, LANES), BF),
            pltpu.VMEM((CHIPS * ROWS, 1024), BF),
            pltpu.VMEM((CHIPS, ROWS, width), BF),
            pltpu.VMEM((CHIPS, ROWS, width), BF),
            pltpu.VMEM((2 * TOK, width), F32),
            pltpu.VMEM((TOK, width), F32),
            pltpu.VMEM((ROWS, width), BF),
            pltpu.VMEM((ROWS, TOK), BF),
            pltpu.VMEM((CHIPS * ROWS, 2 * TOK), BF),
            pltpu.VMEM((2, 256, width), BF),
            pltpu.VMEM((TOK, width), BF),
            dma((17,)), dma((4,)), dma((CHIPS + 1,)), dma((CHIPS + 1,)),
            dma((26 * 2,)), dma((CHIPS, 2)), dma((CHIPS,)), dma((CHIPS,)),
            dma((LAST + 1, 2)), dma((LAST + 1, 2)), dma((LAST + 1, 2)), dma((LAST + 1, 2)),
            dma((LAST + 1, 2)), dma((LAST + 1, 2)), dma((LAST + 1, 2)), dma((LAST + 1, 2)),
            dma((CHIPS,)), dma((CHIPS,)), dma((2,)), dma((2,)), dma((3,)),
        ],
        compiler_params=pltpu.CompilerParams(
            collective_id=0, has_side_effects=True, vmem_limit_bytes=63 * 2**20
        ),
        cost_estimate=pl.CostEstimate(flops=28_200_000_000, bytes_accessed=60_000_000, transcendentals=1_000_000),
    )(
        activations, cotangent, expert_ids.T, combine.T, log_ratio[None], valid_mask[None], segment_ids[None],
        w_gate, w_up, w_down,
    )
    return in_grad, down_grad


def solution(mesh):
    return jax.shard_map(
        local,
        mesh=mesh,
        in_specs=(
            P("expert", "tensor"),
            P("expert", "tensor"),
            P("expert", None),
            P("expert", None),
            P("expert"),
            P("expert"),
            P("expert"),
            P("expert", "tensor", None),
            P("expert", "tensor", None),
            P("expert", None, "tensor"),
        ),
        out_specs=(P("expert", "tensor"), P("expert", None, "tensor")),
        check_vma=False,
    )
```

```python
import functools

import jax
import jax.numpy as jnp
from jax import lax
from jax.experimental import pallas as pl
from jax.experimental.pallas import tpu as pltpu
from jax.sharding import PartitionSpec as P

BF = jnp.bfloat16
F32 = jnp.float32
MESH = pl.DeviceIdType.MESH

SIDE = 4
CHIPS = SIDE * SIDE
CAP = 40
TOK = 128
ROWS = 2 * CAP
TOP = 8
HID = 128
LANES = 3 * HID
BLOCK = 2 * TOK
LAST = 8

ORDER = [
    (0, 0),
    (1, 0), (3, 0),
    (0, 1), (0, 3),
    (1, 3), (1, 1),
    (3, 3), (3, 1),
    (2, 1), (1, 2),
    (3, 2), (2, 3),
    (2, 0), (0, 2),
    (2, 2),
]
CHUNK = [ORDER[:1]] + [ORDER[i : i + 2] for i in range(1, 15, 2)] + [ORDER[15:]]
PASS_ON = {
    (0, "S"): [
        ("full", (0, 0), 1),
    ],
    (0, "P"): [
        ("wait", (3, 0)),
        ("wait", (1, 0)),
    ],
    (1, "L"): [
        ("full", (1, 0), 1),
    ],
    (1, "F"): [
        ("wait", (0, 1)),
        ("half", (3, 0), 0, 1, 0),
        ("wait", (0, 3)),
    ],
    (2, "L"): [
        ("full", (3, 0), 1),
    ],
    (3, "P"): [
        ("wait", (1, 1)),
        ("wait", (1, 3)),
        ("half", (1, 0), 0, -1, 1),
    ],
    (3, "B"): [
        ("half", (1, 1), 1, -1, 1),
    ],
    (3, "L"): [
        ("half", (1, 3), 1, 1, 0),
    ],
    (3, "F"): [
        ("wait", (3, 3)),
    ],
    (4, "P"): [
        ("half", (0, 1), 1, -1, 1),
        ("wait", (3, 1)),
        ("wait", (2, 0)),
    ],
    (4, "S"): [
        ("half", (0, 3), 1, 1, 0),
        ("full", (2, 0), 1),
    ],
    (4, "L"): [
        ("half", (3, 1), 1, -1, 1),
    ],
    (4, "F"): [
        ("wait", (1, 2)),
    ],
    (4, "H"): [
        ("half", (3, 3), 1, 1, 0),
    ],
    (5, "P"): [
        ("wait", (2, 1)),
    ],
    (5, "B"): [
        ("wait", (3, 2)),
    ],
    (5, "L"): [
        ("half", (2, 1), 1, -1, 1),
    ],
    (5, "F"): [
        ("wait", (2, 3)),
    ],
    (6, "F"): [
        ("half", (2, 3), 1, 1, 0),
    ],
    (7, "P"): [
        ("wait", (2, 2)),
        ("wait", (0, 2)),
    ],
}
HALVES = (pl.ds(0, TOK), pl.ds(TOK, BLOCK - TOK))


def first_of(t):
    return max(2 * t - 1, 0) if isinstance(t, int) else 2 * t - lax.div(t + 8, 9)


def dot(a, b, ca, cb):
    return lax.dot_general(a, b, (((ca,), (cb,)), ((), ())), preferred_element_type=F32)


def kernel(
    acts, cots, ids, combine, log_ratio, valid, segments, w_gate, w_up, w_down,
    in_grad, down_grad, gbuf,
    wgu, wd, mine, gext, ext_now, stage, rowact, rowcot, scl, part, own, r1, r2, ag, hs, rets, retr, dense, sibr, late, slate, sall,
    dgt, igt,
    wsem, stsem, xsend, xrecv, gsend, grecv, bsend, brecv, r1s, r1r, r2s, r2r, a1s, a1r, a2s, a2r, rts, rtr,
    css, csr, osem,
):
    e = lax.axis_index("expert")
    x = lax.axis_index("tensor")
    c = lax.rem(e, 2)
    chip = lax.div(e, 2)
    z = lax.div(chip, SIDE)
    y = lax.rem(chip, SIDE)
    width = acts.shape[1]
    right = lax.rem(x + 1, SIDE)
    left = lax.rem(x + SIDE - 1, SIDE)

    def chip_at(dz, dy):
        return lax.rem(z + dz, SIDE) * SIDE + lax.rem(y + dy, SIDE)

    def peer(dz, dy):
        return (chip_at(dz, dy) * 2 + c, x)

    sibling = (chip * 2 + 1 - c, x)

    def zy(da, db):
        return da * (1 - c) + db * c, da * c + db * (1 - c)

    def slot(da, db):
        dz, dy = zy(da % SIDE, db % SIDE)
        return dz * SIDE + dy

    bar = pltpu.get_barrier_semaphore()
    partners = [(e, right), (e, left), sibling]
    partners += [peer(dz, dy) for dz in range(SIDE) for dy in range(SIDE) if (dz, dy) != (0, 0)]
    for p in partners:
        pl.semaphore_signal(bar, inc=1, device_id=p, device_id_type=MESH)

    wcopies = []
    for g in range(8):
        cols = pl.ds(g * HID, HID)
        wcopies.append(
            pltpu.make_async_copy(w_gate.at[0, :, cols], wgu.at[:, pl.ds(2 * g * HID, HID)], wsem.at[2 * g])
        )
        wcopies.append(
            pltpu.make_async_copy(w_up.at[0, :, cols], wgu.at[:, pl.ds((2 * g + 1) * HID, HID)], wsem.at[2 * g + 1])
        )
    wcopies.append(pltpu.make_async_copy(w_down.at[0], wd, wsem.at[16]))
    loads = [
        pltpu.make_async_copy(acts, mine.at[pl.ds(0, TOK)], stsem.at[0]),
        pltpu.make_async_copy(cots, mine.at[pl.ds(TOK, TOK)], stsem.at[1]),
    ]
    for cp in loads:
        cp.start()

    lane = lax.broadcasted_iota(jnp.int32, (TOP, TOK), 1)
    seg = jnp.broadcast_to(segments[...], (TOP, TOK))
    following = pltpu.roll(seg, TOK - 1, 1)
    final_dev = (e + 1) // (2 * CHIPS)
    closing = jnp.where(lane == TOK - 1, final_dev, (following != seg).astype(jnp.int32))
    live = jnp.maximum(jnp.broadcast_to(valid[...], (TOP, TOK)), closing).astype(F32)
    weight = jnp.minimum(jnp.exp(jnp.broadcast_to(log_ratio[...], (TOP, TOK))), 2.0) * live
    slot_scale = (combine[...] * weight).astype(BF)
    count = jnp.broadcast_to(jnp.sum(live, axis=1, keepdims=True), (TOP, TOK)).astype(BF)
    ids_scales = jnp.concatenate([ids[...].astype(F32).astype(BF), slot_scale], axis=0)
    gext[c, 0, :, pl.ds(0, TOK)] = ids_scales
    gext[c, 0, :, pl.ds(TOK, TOK)] = jnp.concatenate([count, count], axis=0)
    for cp in loads:
        cp.wait()
    pl.semaphore_wait(bar, len(partners))

    sends = []

    def block_at(da, db):
        if (da % SIDE, db % SIDE) == (0, 0):
            return mine
        return gbuf.at[c, slot(da, db)]

    def half_copy(n, da, db, axis, by, half):
        na, nb = (da - by, db) if axis == 0 else (da, db - by)
        ta, tb = (by, 0) if axis == 0 else (0, by)
        dz, dy = zy(ta % SIDE, tb % SIDE)
        return pltpu.make_async_remote_copy(
            src_ref=block_at(da, db).at[HALVES[half]],
            dst_ref=gbuf.at[c, slot(na, nb), HALVES[half]],
            send_sem=gsend.at[n],
            recv_sem=grecv.at[slot(na, nb), half],
            device_id=peer(dz, dy),
            device_id_type=MESH,
        )

    def send_half(*what):
        half_copy(len(sends), *what).start()
        sends.append(what)

    def send_full(da, db, axis):
        for by in (1, -1):
            for half in (0, 1):
                send_half(da, db, axis, by, half)

    sib_copies = []

    def sibling_copy(n, da, db):
        return pltpu.make_async_remote_copy(
            src_ref=block_at(da, db),
            dst_ref=gbuf.at[c, slot(da, db)],
            send_sem=bsend.at[n],
            recv_sem=brecv.at[slot(da, db)],
            device_id=sibling,
            device_id_type=MESH,
        )

    def send_sibling(*what):
        sibling_copy(len(sib_copies), *what).start()
        sib_copies.append(what)

    def wait_half(da, db, half):
        ref = gbuf.at[c, slot(da, db), HALVES[half]]
        pltpu.make_async_copy(ref, ref, grecv.at[slot(da, db), half]).wait()

    def act_on(events):
        for kind, at, *rest in events:
            if kind == "wait":
                wait_half(*at, 0)
                wait_half(*at, 1)
                send_sibling(*at)
            elif kind == "full":
                send_full(*at, *rest)
            else:
                send_half(*at, *rest)

    def ext_copy(dz, dy):
        n = dz * SIDE + dy
        to = (-dz % SIDE) * SIDE + -dy % SIDE
        return pltpu.make_async_remote_copy(
            src_ref=gext.at[c, 0], dst_ref=gext.at[c, to], send_sem=xsend.at[n], recv_sem=xrecv.at[to],
            device_id=sibling if n == 0 else peer(dz, dy), device_id_type=MESH,
        )

    def ext_relay():
        others = gext.at[c, pl.ds(1, CHIPS - 1)]
        return pltpu.make_async_remote_copy(
            src_ref=others, dst_ref=others, send_sem=xsend.at[CHIPS], recv_sem=xrecv.at[CHIPS],
            device_id=sibling, device_id_type=MESH,
        )

    offsets = [(dz, dy) for dz in range(SIDE) for dy in range(SIDE)]
    send_full(0, 0, 0)
    ext_copy(0, 0).start()
    send_sibling(0, 0)
    for cp in wcopies:
        cp.start()
    for at in offsets[1:]:
        ext_copy(*at).start()

    row_i = lax.broadcasted_iota(jnp.int32, (TOK, TOK), 0)
    col_i = lax.broadcasted_iota(jnp.int32, (TOK, TOK), 1)
    upper = (row_i < col_i).astype(BF)
    slot_iota = lax.broadcasted_iota(jnp.int32, (ROWS, TOK), 0).astype(F32)

    def routing(ext, expert, core):
        hit = (ext[0:TOP] == expert).astype(F32)
        mask = jnp.sum(hit, axis=0, keepdims=True)
        scale = jnp.sum(hit * ext[TOP : 2 * TOP], axis=0, keepdims=True)
        rank = dot(jnp.broadcast_to(mask, (16, TOK)).astype(BF), upper, 1, 0)[0:1]
        key = jnp.where(mask > 0.5, rank + float(CAP * core), -1.0)
        return (slot_iota == key).astype(F32), scale

    def remote_x(src, dst, ssem, rsem, to):
        return pltpu.make_async_remote_copy(
            src_ref=src, dst_ref=dst, send_sem=ssem, recv_sem=rsem, device_id=(e, to), device_id_type=MESH
        )

    def rs1(t, n, h):
        return remote_x(
            part.at[lax.rem(t, 3), pl.ds(0, n), 1, h], r1.at[pl.ds(first_of(t), n), h],
            r1s.at[t, h], r1r.at[t, h], (right, left)[h],
        )

    def rs2(t, n, side):
        return remote_x(
            part.at[lax.rem(t, 3), pl.ds(0, n), 2 * side], r2.at[pl.ds(first_of(t), n), side],
            r2s.at[t, side], r2r.at[t, side], (right, left)[side],
        )

    def ag1(t, n, side):
        ref = ag.at[pl.ds(first_of(t), n), pl.ds(2 * x, 2)]
        return remote_x(ref, ref, a1s.at[t, side], a1r.at[t, side], (right, left)[side])

    def ag1_wait(t, n, side):
        ref = ag.at[pl.ds(first_of(t), n), pl.ds(2 * (left, right)[side], 2)]
        pltpu.make_async_copy(ref, ref, a1r.at[t, side]).wait()

    def ag2(t, n, side):
        ref = ag.at[pl.ds(first_of(t), n), 2 * (left, right)[side] + side]
        return remote_x(ref, ref, a2s.at[t, side], a2r.at[t, side], (right, left)[side])

    def ag2_wait(t, n, side):
        ref = ag.at[pl.ds(first_of(t), n), 2 * lax.rem(x + 2, SIDE) + side]
        pltpu.make_async_copy(ref, ref, a2r.at[t, side]).wait()

    def ret_copy(k):
        dz, dy = ORDER[k]
        if k == 0:
            return pltpu.make_async_copy(rets.at[0], retr.at[0], rtr.at[0])
        return pltpu.make_async_remote_copy(
            src_ref=rets.at[k], dst_ref=retr.at[k], send_sem=rts.at[k], recv_sem=rtr.at[k],
            device_id=peer(dz, dy), device_id_type=MESH,
        )

    def load_stage(elements):
        copies = []
        for i, at in enumerate(elements):
            da, db = at
            if at != (0, 0):
                ext_now[i, 0] = gext[0, da * SIDE + db, :, pl.ds(0, TOK)]
                ext_now[i, 1] = gext[1, db * SIDE + da, :, pl.ds(0, TOK)]
            theirs = (da * c + db * (1 - c)) * SIDE + da * (1 - c) + db * c
            ref = gbuf.at[1 - c, theirs]
            pltpu.make_async_copy(ref, ref, brecv.at[theirs]).wait()
            copies.append(pltpu.make_async_copy(block_at(*at), stage.at[i, c], stsem.at[2 * i]))
            copies.append(pltpu.make_async_copy(ref, stage.at[i, 1 - c], stsem.at[2 * i + 1]))
        for cp in copies:
            cp.start()
        for cp in copies:
            cp.wait()

    def sends_done(t, n):
        for h in range(2):
            rs1(t, n, h).wait_send()
            rs2(t, n, h).wait_send()

    def forward(t, n):
        first = first_of(t)
        expert = e.astype(F32)
        for i in range(n):
            picks, scales = [], []
            for core in range(2):
                pick, scale = routing(ext_now[i, core].astype(F32), expert, core)
                picks.append(pick)
                scales.append(jnp.sum(pick * scale, axis=1, keepdims=True))
            pick = jnp.concatenate(picks, axis=1).astype(BF)
            rows = pl.ds(pl.multiple_of((first + i) * ROWS, 16), ROWS)
            scl[first + i] = jnp.broadcast_to(scales[0] + scales[1], (ROWS, HID))
            act = jnp.concatenate([stage[i, 0, pl.ds(0, TOK), :], stage[i, 1, pl.ds(0, TOK), :]], axis=0)
            rowact[pl.ds(i * ROWS, ROWS), :] = dot(pick, act, 1, 0).astype(BF)
            cot = jnp.concatenate([stage[i, 0, pl.ds(TOK, TOK), :], stage[i, 1, pl.ds(TOK, TOK), :]], axis=0)
            rowcot[rows, :] = dot(pick, cot, 1, 0).astype(BF)

        at = lax.rem(t, 3)
        chunk_rows = pl.ds(pl.multiple_of(first * ROWS, 16), n * ROWS)
        for j in (2, 1, 3, 0):
            a = lax.rem(x + j, SIDE)
            gu = dot(rowact[pl.ds(0, n * ROWS), :], wgu[:, pl.ds(pl.multiple_of(a * 512, 512), 512)], 1, 0)
            d = dot(rowcot[chunk_rows, :], wd[pl.ds(pl.multiple_of(a * 256, 256), 256), :], 1, 1)
            for i in range(n):
                for h in range(2):
                    gu_h = gu[i * ROWS : (i + 1) * ROWS, 256 * h : 256 * h + 256]
                    d_h = d[i * ROWS : (i + 1) * ROWS, HID * h : HID * h + HID]
                    if j == 0:
                        own[at, i, h, :, pl.ds(0, 256)] = gu_h
                        own[at, i, h, :, pl.ds(256, HID)] = d_h
                    else:
                        part[at, i, j - 1, h, :, pl.ds(0, 256)] = gu_h.astype(BF)
                        part[at, i, j - 1, h, :, pl.ds(256, HID)] = d_h.astype(BF)
            if j == 2:
                rs1(t, n, 0).start()
                rs1(t, n, 1).start()

    def pass_sums(t, n):
        at = lax.rem(t, 3)
        first = first_of(t)
        for h in range(2):
            rs1(t, n, h).wait_recv()
            for i in range(n):
                part[at, i, 2 * h, h] = (part[at, i, 2 * h, h].astype(F32) + r1[first + i, h].astype(F32)).astype(BF)
            rs2(t, n, h).start()

    def pointwise(t, n):
        at = lax.rem(t, 3)
        first = first_of(t)
        rs2(t, n, 0).wait_recv()
        rs2(t, n, 1).wait_recv()
        for i in range(n):
            scale = scl[first + i]
            for h in range(2):
                v = own[at, i, h] + r2[first + i, 0, h].astype(F32) + r2[first + i, 1, h].astype(F32)
                gate, up, down = v[:, :HID], v[:, HID : 2 * HID], v[:, 2 * HID :]
                sig = jax.nn.sigmoid(gate)
                act = gate * sig
                slope = sig * (1.0 + gate * (1.0 - sig))
                dh = down * scale
                g = 2 * x + h
                ag[first + i, g, :, pl.ds(0, HID)] = (dh * up * slope).astype(BF)
                ag[first + i, g, :, pl.ds(HID, HID)] = (dh * act).astype(BF)
                ag[first + i, g, :, pl.ds(2 * HID, HID)] = (act * up * scale).astype(BF)
        ag1(t, n, 0).start()
        ag1(t, n, 1).start()

    def pass_shares(t, n):
        for side in range(2):
            ag1_wait(t, n, side)
            ag2(t, n, side).start()

    def backward(t, n):
        ag2_wait(t, n, 0)
        ag2_wait(t, n, 1)
        first = first_of(t)
        grads = []
        for i in range(n):
            rows = pl.ds(pl.multiple_of((first + i) * ROWS, 16), ROWS)
            for g in range(8):
                hs[rows, pl.ds(g * HID, HID)] = ag[first + i, g, :, pl.ds(2 * HID, HID)]
            grads.append(jnp.concatenate([ag[first + i, g, :, pl.ds(0, 2 * HID)] for g in range(8)], axis=1))
        grads = jnp.concatenate(grads, axis=0) if n > 1 else grads[0]
        rowact[pl.ds(0, n * ROWS), :] = dot(grads, wgu[...], 1, 1).astype(BF)

        core0 = lax.broadcasted_iota(jnp.int32, (ROWS, width), 0) < CAP
        for k, elements in enumerate(CHUNK):
            if len(elements) != n:
                continue

            @pl.when(t == k)
            def _():
                for i, (da, db) in enumerate(elements):
                    k0, k1 = ORDER.index((da, db)), ORDER.index((db, da))
                    out = rowact[pl.ds(i * ROWS, ROWS), :]
                    if k0 < k1:
                        rets[k0] = out
                        rets[k1] = out
                    elif k0 == k1:
                        rets[k0] = out
                        ret_copy(k0).start()
                    else:
                        wide = out.astype(F32)
                        rets[k0] = jnp.where(core0, wide, rets[k0].astype(F32)).astype(BF)
                        rets[k1] = jnp.where(core0, rets[k1].astype(F32), wide).astype(BF)
                        ret_copy(k0).start()
                        ret_copy(k1).start()

    def on(cond, f, *args):
        @pl.when(cond)
        def _():
            f(*args)

    def any_size(t, f):
        on((t >= 1) & (t < LAST), f, t, 2)
        on(t == LAST, f, t, 1)

    def after(s, op):
        for k, name in PASS_ON:
            if name != op or (k == 0) != isinstance(s, int):
                continue
            if k == 0:
                act_on(PASS_ON[k, name])
            else:
                on(s == k, act_on, PASS_ON[k, name])

    load_stage(CHUNK[0])
    own_ext = gext.at[1 - c, 0]
    pltpu.make_async_copy(own_ext, own_ext, xrecv.at[0]).wait()
    ext_now[0] = gext[:, 0, :, pl.ds(0, TOK)]
    after(0, "L")
    for cp in wcopies:
        cp.wait()
    forward(0, 1)
    after(0, "F")
    for n in range(1, CHIPS):
        ref = gext.at[c, n]
        pltpu.make_async_copy(ref, ref, xrecv.at[n]).wait()
    ext_relay().start()
    pass_sums(0, 1)
    after(0, "S")
    pointwise(0, 1)
    after(0, "P")
    for core in range(2):
        ext = ext_now[0, core].astype(F32)
        for k, (dz, dy) in enumerate(ORDER):
            expert = (2 * chip_at(-dz % SIDE, -dy % SIDE) + c).astype(F32)
            pick, _ = routing(ext, expert, core)
            sall[pl.ds(k * ROWS, ROWS), pl.ds(core * TOK, TOK)] = pick.astype(BF)
    dz, dy = ORDER[-1]
    twin = (2 * chip_at(-dz % SIDE, -dy % SIDE) + 1 - c).astype(F32)
    pick0, _ = routing(ext_now[0, 0].astype(F32), twin, 0)
    pick1, _ = routing(ext_now[0, 1].astype(F32), twin, 1)
    slate[...] = jnp.where(c == 0, pick0, pick1).astype(BF)
    after(0, "sall")
    ext_relay().wait_recv()

    def step(s, carry):
        any_size(s - 2, pointwise)
        after(s, "P")
        any_size(s - 1, pass_sums)
        after(s, "S")
        on((s >= 4) & (s < LAST + 3), backward, s - 3, 2)
        on((s == 3) | (s == LAST + 3), backward, s - 3, 1)
        after(s, "B")
        for k in range(1, LAST + 1):
            on(s == k, load_stage, CHUNK[k])
        after(s, "L")
        on(s == 3, sends_done, 0, 1)
        on((s >= 4) & (s <= LAST), sends_done, s - 3, 2)
        any_size(s, forward)
        after(s, "F")
        on(s == 2, pass_shares, 0, 1)
        any_size(s - 2, pass_shares)
        after(s, "H")
        return carry

    lax.fori_loop(1, LAST + 4, step, 0)

    live_total = jnp.zeros((2 * TOP, TOK), F32)
    for core in range(2):
        for n in range(CHIPS):
            live_total += gext[core, n, :, pl.ds(TOK, TOK)].astype(F32)
    factor = float(2 * CHIPS * TOK) / live_total[0:1, 0:1]
    outs = []
    for f in range(4):
        if f >= 2:
            outs[f - 2].wait()
        dgt[f % 2] = (dot(hs[:, pl.ds(256 * f, 256)], rowcot[...], 0, 0) * factor).astype(BF)
        cp = pltpu.make_async_copy(dgt.at[f % 2], down_grad.at[0, pl.ds(256 * f, 256), :], osem.at[f % 2])
        cp.start()
        outs.append(cp)

    def returned(k):
        pltpu.make_async_copy(retr.at[k], retr.at[k], rtr.at[k]).wait()

    for k in range(CHIPS - 1):
        returned(k)
    early = (CHIPS - 1) * ROWS
    dense[...] = dot(sall[pl.ds(0, early), :], retr[pl.ds(0, CHIPS - 1)].reshape(early, width), 0, 0)
    swap = pltpu.make_async_remote_copy(
        src_ref=dense.at[pl.ds(pl.multiple_of((1 - c) * TOK, TOK), TOK)],
        dst_ref=sibr,
        send_sem=css.at[0],
        recv_sem=csr.at[0],
        device_id=sibling,
        device_id_type=MESH,
    )
    swap.start()
    returned(CHIPS - 1)
    relay = pltpu.make_async_remote_copy(
        src_ref=retr.at[CHIPS - 1],
        dst_ref=late,
        send_sem=css.at[1],
        recv_sem=csr.at[1],
        device_id=sibling,
        device_id_type=MESH,
    )
    relay.start()
    own_lanes = pl.ds(pl.multiple_of(c * TOK, TOK), TOK)
    total = dense[own_lanes, :] + dot(sall[pl.ds(early, ROWS), own_lanes], retr[CHIPS - 1], 0, 0)
    swap.wait()
    relay.wait()
    total = total + sibr[...] + dot(slate[...], late[...], 0, 0)
    igt[...] = (total * factor).astype(BF)
    final = pltpu.make_async_copy(igt, in_grad, osem.at[2])
    final.start()

    final.wait()
    outs[2].wait()
    outs[3].wait()
    for n, what in enumerate(sends):
        half_copy(n, *what).wait_send()
    for n, what in enumerate(sib_copies):
        sibling_copy(n, *what).wait_send()
    for k in range(1, CHIPS):
        ret_copy(k).wait_send()

    for at in offsets:
        ext_copy(*at).wait_send()
    ext_relay().wait_send()
    for t in (6, 7):
        sends_done(t, 2)
    sends_done(LAST, 1)

    def drain(t, n):
        for h in range(2):
            ag1(t, n, h).wait_send()
            ag2(t, n, h).wait_send()

    def drain_pair(t, carry):
        drain(t, 2)
        return carry

    drain(0, 1)
    lax.fori_loop(1, LAST, drain_pair, 0)
    drain(LAST, 1)


def local(
    activations, cotangent, expert_ids, combine, log_ratio, valid_mask, segment_ids, w_gate, w_up, w_down
):
    tok_rows, width = activations.shape
    any_spec = pl.BlockSpec(memory_space=pl.ANY)
    dma = pltpu.SemaphoreType.DMA
    in_grad, down_grad, _ = pl.pallas_call(
        kernel,
        out_shape=(
            jax.ShapeDtypeStruct((tok_rows, width), BF),
            jax.ShapeDtypeStruct(w_down.shape, BF),
            jax.ShapeDtypeStruct((2, CHIPS, BLOCK, width), BF),
        ),
        in_specs=[any_spec] * 2 + [pl.BlockSpec(memory_space=pltpu.VMEM)] * 5 + [any_spec] * 3,
        out_specs=(any_spec,) * 3,
        scratch_shapes=[
            pltpu.VMEM((width, 2048), BF),
            pltpu.VMEM((1024, width), BF),
            pltpu.VMEM((BLOCK, width), BF),
            pltpu.VMEM((2, CHIPS, 2 * TOP, 2 * TOK), BF),
            pltpu.VMEM((2, 2, 2 * TOP, TOK), BF),
            pltpu.VMEM((2, 2, BLOCK, width), BF),
            pltpu.VMEM((2 * ROWS, width), BF),
            pltpu.VMEM((CHIPS * ROWS, width), BF),
            pltpu.VMEM((CHIPS, ROWS, HID), F32),
            pltpu.VMEM((3, 2, 3, 2, ROWS, LANES), BF),
            pltpu.VMEM((3, 2, 2, ROWS, LANES), F32),
            pltpu.VMEM((CHIPS, 2, ROWS, LANES), BF),
            pltpu.VMEM((CHIPS, 2, 2, ROWS, LANES), BF),
            pltpu.VMEM((CHIPS, 8, ROWS, LANES), BF),
            pltpu.VMEM((CHIPS * ROWS, 1024), BF),
            pltpu.VMEM((CHIPS, ROWS, width), BF),
            pltpu.VMEM((CHIPS, ROWS, width), BF),
            pltpu.VMEM((2 * TOK, width), F32),
            pltpu.VMEM((TOK, width), F32),
            pltpu.VMEM((ROWS, width), BF),
            pltpu.VMEM((ROWS, TOK), BF),
            pltpu.VMEM((CHIPS * ROWS, 2 * TOK), BF),
            pltpu.VMEM((2, 256, width), BF),
            pltpu.VMEM((TOK, width), BF),
            dma((17,)), dma((4,)), dma((CHIPS + 1,)), dma((CHIPS + 1,)),
            dma((26 * 2,)), dma((CHIPS, 2)), dma((CHIPS,)), dma((CHIPS,)),
            dma((LAST + 1, 2)), dma((LAST + 1, 2)), dma((LAST + 1, 2)), dma((LAST + 1, 2)),
            dma((LAST + 1, 2)), dma((LAST + 1, 2)), dma((LAST + 1, 2)), dma((LAST + 1, 2)),
            dma((CHIPS,)), dma((CHIPS,)), dma((2,)), dma((2,)), dma((3,)),
        ],
        compiler_params=pltpu.CompilerParams(
            collective_id=0, has_side_effects=True, vmem_limit_bytes=63 * 2**20
        ),
        cost_estimate=pl.CostEstimate(flops=28_200_000_000, bytes_accessed=60_000_000, transcendentals=1_000_000),
    )(
        activations, cotangent, expert_ids.T, combine.T, log_ratio[None], valid_mask[None], segment_ids[None],
        w_gate, w_up, w_down,
    )
    return in_grad, down_grad


def solution(mesh):
    return jax.shard_map(
        local,
        mesh=mesh,
        in_specs=(
            P("expert", "tensor"),
            P("expert", "tensor"),
            P("expert", None),
            P("expert", None),
            P("expert"),
            P("expert"),
            P("expert"),
            P("expert", "tensor", None),
            P("expert", "tensor", None),
            P("expert", None, "tensor"),
        ),
        out_specs=(P("expert", "tensor"), P("expert", None, "tensor")),
        check_vma=False,
    )
```
